512 devices in a mesh: space: 32 (over y, z_lo), replica: 16 (over z_hi, x, core).
Axes of the slice: x: 4, y: 8, z: 8 (z_hi: 2, z_lo: 4; z = z_hi * 4 + z_lo), core: 2. Of those that a mesh axis runs over, the one named last changes fastest.
Arguments:
- volumes: bfloat16 [16, 32, 2, 8, 16, 256], P('replica', 'space'), may hold values from -6 to 6
- weights: bfloat16 [3, 3, 3, 256, 128], replicated, may hold values from -0.078125 to 0.078125
- out_grads: bfloat16 [16, 32, 2, 8, 16, 128], P('replica', 'space'), may hold values from -6 to 6
Outputs:
- outputs: bfloat16 [16, 32, 2, 8, 16, 128], P('replica', 'space')
- in_grads: bfloat16 [16, 32, 2, 8, 16, 256], P('replica', 'space')
- kernel_grad: float32 [3, 3, 3, 256, 128], P(None, None, None, 'replica')
The draws below stay inside these ranges and needn't reach their ends.
All inputs are finite; a program needn't handle non-finite values.
Results may differ from the reference program's by a relative error of at most 0.001.
Values may be sent and summed in bfloat16 or wider, within the bound.
A program may use at most 64 MiB of HBM per device.

```python
import jax
import jax.numpy as jnp
from jax import lax

CIN = 256
COUT = 128
BX = 2
BY = 8
BZ = 16
VOLUMES = 16
BLOCKS = 32
TOTAL = 131072


def shard_levels(key, extent, cuts, smallest, high):
    level, own = 1.0, jax.random.fold_in(key, 6)
    for dim, shards_of in cuts:
        draws = jnp.exp(jax.random.uniform(jax.random.fold_in(own, dim), (shards_of,), jnp.float32, smallest / len(cuts), high / len(cuts)))
        level = level * jnp.repeat(draws, extent[dim] // shards_of).reshape([-1 if axis == dim else 1 for axis in range(len(extent))])
    return level


def scatter_about(rng, shape, width, reach, pieces=(), held_as=jnp.bfloat16):
    entries = jax.random.normal(rng, shape, jnp.float32) * width
    if len(pieces) > 0:
        entries = shard_levels(rng, shape, pieces, -0.22, 0.18) * entries
    return jnp.clip(entries, min=-reach, max=reach).astype(held_as)


def setup_inputs(seed: int = 0) -> dict:
    key_of = jax.random.split(jax.random.key(seed), 4)
    volumes = scatter_about(key_of[0], (VOLUMES, BLOCKS, BX, BY, BZ, CIN), 1.0, 6.0, ((0, 16), (1, 32)))
    weights = scatter_about(key_of[1], (3, 3, 3, CIN, COUT), (27 * CIN) ** -0.5, 0.078125)
    out_grads = scatter_about(key_of[2], (VOLUMES, BLOCKS, BX, BY, BZ, COUT), 1.0, 6.0, ((0, 16), (1, 32)))
    return dict(volumes=volumes, weights=weights, out_grads=out_grads)


def to_volume(blocks):
    chans = blocks.shape[-1]
    grid_x = blocks.shape[0] // 8
    shaped = blocks.reshape(grid_x, 4, 2, BX, BY, BZ, chans)
    return shaped.transpose(0, 3, 1, 4, 2, 5, 6).reshape(grid_x * BX, 4 * BY, 2 * BZ, chans)

def to_blocks(volume):
    chans = volume.shape[-1]
    grid_x = volume.shape[0] // BX
    shaped = volume.reshape(grid_x, BX, 4, BY, 2, BZ, chans)
    return shaped.transpose(0, 2, 4, 1, 3, 5, 6).reshape(grid_x * 8, BX, BY, BZ, chans)

def pad_cells(field):
    return jnp.pad(field, ((1, 1), (1, 1), (1, 1), (0, 0)))

def windows(padded, row_tap, col_tap):
    size_x = padded.shape[0] - 2
    size_y = padded.shape[1] - 2
    size_z = padded.shape[2] - 2
    parts = [padded[row_tap:row_tap + size_x, col_tap:col_tap + size_y, depth:depth + size_z] for depth in range(3)]
    joined = jnp.concatenate(parts, axis=-1)
    return joined.reshape(size_x * size_y * size_z, 3 * padded.shape[3])

def convolve(padded, kernel):
    chans_in = kernel.shape[3]
    chans_out = kernel.shape[4]
    shape_out = (padded.shape[0] - 2, padded.shape[1] - 2, padded.shape[2] - 2, chans_out)
    total = jnp.zeros((shape_out[0] * shape_out[1] * shape_out[2], chans_out), jnp.float32)
    for row_tap in range(3):
        for col_tap in range(3):
            window = windows(padded, row_tap, col_tap)
            total = total + jnp.dot(window, kernel[row_tap, col_tap].reshape(3 * chans_in, chans_out), preferred_element_type=jnp.float32)
    return total.reshape(shape_out)

def kernel_terms(padded, grads):
    chans_in = padded.shape[3]
    flat_grads = grads.reshape(-1, grads.shape[-1])
    rows = []
    for row_tap in range(3):
        cols = []
        for col_tap in range(3):
            window = windows(padded, row_tap, col_tap)
            term = jnp.dot(window.T, flat_grads, preferred_element_type=jnp.float32)
            cols.append(term.reshape(3, chans_in, flat_grads.shape[1]))
        rows.append(jnp.stack(cols, axis=0))
    return jnp.stack(rows, axis=0)

def reference(volumes, weights, out_grads):
    flipped = jnp.flip(weights, axis=(0, 1, 2)).transpose(0, 1, 2, 4, 3)

    def one_volume(carry, pair):
        blocks, grad_blocks = pair
        padded = pad_cells(to_volume(blocks))
        grad_volume = to_volume(grad_blocks)
        result = convolve(padded, weights).astype(jnp.bfloat16)
        back = convolve(pad_cells(grad_volume), flipped).astype(jnp.bfloat16)
        carry = carry + kernel_terms(padded, grad_volume)
        return (carry, (to_blocks(result), to_blocks(back)))
    start = jnp.zeros((3, 3, 3, CIN, COUT), jnp.float32)
    summed, (outputs, in_grads) = lax.scan(one_volume, start, (volumes, out_grads))
    kernel_grad = summed / jnp.sqrt(jnp.float32(TOTAL))
    return (outputs, in_grads, kernel_grad)
```

```python
import jax
import jax.numpy as jnp
from jax import lax
from jax.experimental import pallas as pl
from jax.experimental.pallas import tpu as pltpu
from jax.sharding import PartitionSpec as P

MESH = pl.DeviceIdType.MESH
F32 = jnp.float32
BF16 = jnp.bfloat16
GROUPS = 7
LIFT = 32768.0
PLANE = [(ox, oy) for ox in (-1, 0, 1) for oy in (-1, 0, 1)]
SIDES = [o for o in PLANE if o != (0, 0)]


def encode(u, msg):
    n = u.shape[0]
    top = jnp.max(jnp.max(jnp.abs(u), axis=0), axis=0, keepdims=True)
    top = jnp.maximum(top, 1e-30).astype(BF16)
    v = u * (LIFT / top.astype(F32))
    v2 = v * v
    v4 = v2 * v2
    msg[pl.ds(0, n)] = ((v4 * v2) * (v * jnp.abs(v))).astype(BF16)
    msg[n] = jnp.broadcast_to(top.astype(F32), (16, 128)).astype(BF16)


def decode(msg, n):
    y = msg[pl.ds(0, n)].astype(F32)
    scale = msg[n].astype(F32) * (1.0 / LIFT)
    a = jnp.abs(y)
    t = lax.rsqrt(lax.rsqrt(a))
    u = jnp.where(a == 0.0, 0.0, t * lax.rsqrt(t))
    return jnp.where(y < 0.0, -u, u) * scale


def kernel(
    x_hbm, w_hbm, g_hbm, out_hbm, back_hbm, kg_hbm,
    wv, xc, gc, x3, g3, xface, gface, xfr, gfr, xt,
    part, sib_recv, x_send, x_recv, own, y_send, y_recv, z_own, z_send, z_recv, kg,
    acc_f, acc_b, out_v, back_v,
    in_sem, out_sem, halo_s, halo_r, sib_s, sib_r, xs_s, xs_r, ys_s, ys_r, zs_s, zs_r, ag_s, ag_r,
):
    s = lax.axis_index("space")
    r = lax.axis_index("replica")
    y, zl = s // 4, s % 4
    zh, x, c = r // 8, (r // 2) % 4, r % 2
    gx, gy, gz = s // 8, (s // 2) % 4, s % 2

    loads = [
        pltpu.make_async_copy(g_hbm, gc.at[pl.ds(1, 2), pl.ds(1, 8)], in_sem.at[0]),
        pltpu.make_async_copy(x_hbm, xc.at[pl.ds(1, 2), pl.ds(1, 8)], in_sem.at[1]),
        pltpu.make_async_copy(w_hbm, wv, in_sem.at[2]),
    ]
    for load in loads:
        load.start()
    for field in (gc, xc):
        z = jnp.zeros((1, 10, 16, field.shape[3]), BF16)
        field[pl.ds(0, 1)] = z
        field[pl.ds(3, 1)] = z
        z = jnp.zeros((2, 1, 16, field.shape[3]), BF16)
        field[pl.ds(1, 2), pl.ds(0, 1)] = z
        field[pl.ds(1, 2), pl.ds(9, 1)] = z
    gfr[...] = jnp.zeros_like(gfr)
    xfr[...] = jnp.zeros_like(xfr)

    def inside(ox, oy):
        return (gx + ox >= 0) & (gx + ox <= 3) & (gy + oy >= 0) & (gy + oy <= 3)

    def at(ox, oy, other):
        return ((gx + ox) * 8 + (gy + oy) * 2 + (1 - gz if other else gz), r)

    sibling = (s, r + 1 - 2 * c)
    x_peers = [(s, zh * 8 + ((x + d) % 4) * 2 + c) for d in (1, 2, 3)]
    y_peers = [(((y + d) % 8) * 4 + zl, r) for d in range(1, 8)]

    def z_peer(d):
        z_to = (zh * 4 + zl + d) % 8
        return (y * 4 + z_to % 4, (z_to // 4) * 8 + x * 2 + c)

    z_peers = [z_peer(d) for d in range(1, 8)]

    barrier = pltpu.get_barrier_semaphore()

    def greet(who):
        pl.semaphore_signal(barrier, inc=1, device_id=who, device_id_type=MESH)

    greet(sibling)
    for who in x_peers + y_peers + z_peers:
        greet(who)
    expected = 18
    for ox, oy in PLANE:
        here = inside(ox, oy)
        if (ox, oy) == (0, 0):
            greet(at(0, 0, True))
            expected = expected + 1
            continue

        @pl.when(here)
        def _(ox=ox, oy=oy):
            greet(at(ox, oy, False))
            greet(at(ox, oy, True))

        expected = expected + jnp.where(here, 2, 0)

    def cut(o, size):
        return (pl.ds(1, size), pl.ds(1, size)) if o == 0 else (
            (pl.ds(size, 1), pl.ds(0, 1)) if o == 1 else (pl.ds(1, 1), pl.ds(size + 1, 1)))

    def slab(field, k, ox, oy, base):
        (xs, xd), (ys, yd) = cut(ox, 2), cut(oy, 8)
        return pltpu.make_async_remote_copy(
            field.at[xs, ys], field.at[xd, yd], halo_s.at[base + k], halo_r.at[base + k],
            device_id=at(ox, oy, False), device_id_type=MESH)

    def face(src, dst, k, ox, oy, base):
        return pltpu.make_async_remote_copy(
            src, dst.at[1 - ox, 1 - oy], halo_s.at[base + k], halo_r.at[base + k],
            device_id=at(ox, oy, True), device_id_type=MESH)

    def halo(field, fsrc, fdst, base, do):
        for k, (ox, oy) in enumerate(SIDES):
            here = inside(-ox, -oy) if do == "recv" else inside(ox, oy)

            @pl.when(here)
            def _(k=k, ox=ox, oy=oy):
                one = slab(field, k, ox, oy, base)
                two = face(fsrc, fdst, 8 + k, ox, oy, base)
                if do == "start":
                    one.start()
                    two.start()
                elif do == "recv":
                    one.wait_recv()
                    two.wait_recv()
                else:
                    one.wait_send()
                    two.wait_send()
        own_face = face(fsrc, fdst, 16, 0, 0, base)
        {"start": own_face.start, "recv": own_face.wait_recv, "send": own_face.wait_send}[do]()

    rows = lax.broadcasted_iota(jnp.int32, (16, 256), 0)
    cols = lax.broadcasted_iota(jnp.int32, (16, 256), 1)
    pick = jnp.where(cols == rows * 16 + jnp.where(gz == 0, 15, 0), 1.0, 0.0).astype(BF16)

    def interior(field):
        return field[pl.ds(1, 2), pl.ds(1, 8)].reshape(256, field.shape[3])

    loads[0].wait()
    gface[...] = jnp.dot(pick, interior(gc), preferred_element_type=F32).astype(BF16)
    pl.semaphore_wait(barrier, expected)
    halo(gc, gface, gfr, 0, "start")
    loads[1].wait()
    xface[...] = jnp.dot(pick, interior(xc), preferred_element_type=F32).astype(BF16)
    halo(xc, xface, xfr, 17, "start")
    xt[...] = interior(xc).T

    def shift_all(field, received, shifted):
        ch = field.shape[3]
        shifted[1] = field[...]
        ri = lax.broadcasted_iota(jnp.int32, (160, 208), 0)
        ci = lax.broadcasted_iota(jnp.int32, (160, 208), 1)
        zi, yi = ri % 16, ri // 16
        for layer in range(4):
            ox = (0, 1, 1, 2)[layer]
            xrow = (8, 0, 8, 0)[layer]
            face_row = jnp.where(yi == 0, 160 + xrow + 7, jnp.where(yi == 9, 192 + xrow, 176 + xrow + yi - 1))
            low_col = jnp.where(zi > 0, ri - 1, jnp.where(gz == 1, face_row, -1))
            high_col = jnp.where(zi < 15, ri + 1, jnp.where(gz == 0, face_row, -1))
            low = jnp.where(ci == low_col, 1.0, 0.0).astype(BF16)
            high = jnp.where(ci == high_col, 1.0, 0.0).astype(BF16)
            cells = jnp.concatenate([field[layer].reshape(160, ch), received[ox].reshape(48, ch)], axis=0)
            shifted[0, layer] = jnp.dot(low, cells, preferred_element_type=F32).astype(BF16).reshape(10, 16, ch)
            shifted[2, layer] = jnp.dot(high, cells, preferred_element_type=F32).astype(BF16).reshape(10, 16, ch)

    def tap_of(t):
        t = jnp.minimum(t, 26)
        return t // 9, (t // 3) % 3, t % 3

    def g_window(t):
        dx, dy, dz = tap_of(t)
        return g3[2 - dz, pl.ds(2 - dx, 2), pl.ds(2 - dy, 8)].reshape(256, 128)

    def x_window(t):
        dx, dy, dz = tap_of(t)
        return x3[dz, pl.ds(dx, 2), pl.ds(dy, 8)].reshape(256, 256)

    halo(gc, gface, gfr, 0, "recv")
    shift_all(gc, gfr, g3)

    def to_sibling(g):
        return pltpu.make_async_remote_copy(
            part.at[g, :, :, :, 1 - c], sib_recv.at[g], sib_s.at[g], sib_r.at[g],
            device_id=sibling, device_id_type=MESH)

    def to_x(g, d):
        return pltpu.make_async_remote_copy(
            x_send.at[g, d - 1], x_recv.at[g, d - 1], xs_s.at[g, d - 1], xs_r.at[g, d - 1],
            device_id=x_peers[d - 1], device_id_type=MESH)

    def to_y(g):
        slot = (g - y + 8) % 8 - 1
        return pltpu.make_async_remote_copy(
            y_send.at[g], y_recv.at[slot], ys_s.at[g], ys_r.at[slot],
            device_id=(g * 4 + zl, r), device_id_type=MESH)

    def from_y(slot):
        return pltpu.make_async_remote_copy(
            y_send.at[0], y_recv.at[slot], ys_s.at[0], ys_r.at[slot],
            device_id=y_peers[0], device_id_type=MESH)

    def to_z(d):
        z_to = (zh * 4 + zl + d) % 8
        return pltpu.make_async_remote_copy(
            z_send.at[z_to // 4], z_recv.at[d - 1], zs_s.at[d - 1], zs_r.at[d - 1],
            device_id=z_peers[d - 1], device_id_type=MESH)

    def gather(d):
        return pltpu.make_async_remote_copy(
            kg.at[y], kg.at[y], ag_s.at[d - 1], ag_r.at[y],
            device_id=y_peers[d - 1], device_id_type=MESH)

    def gathered(g):
        return pltpu.make_async_remote_copy(
            kg.at[g], kg.at[g], ag_s.at[0], ag_r.at[g],
            device_id=y_peers[0], device_id_type=MESH)

    def pair_sum(g, xx):
        mine = part[g, :, :, pl.ds(xx, 1), pl.ds(c, 1)].reshape(8, 16, 128)
        return mine + sib_recv[g, :, :, pl.ds(xx, 1)].reshape(8, 16, 128)

    def send_x(g):
        to_sibling(g).wait_recv()
        for d in (2, 1, 3):
            encode(pair_sum(g, (x + d) % 4), x_send.at[g, d - 1])
            to_x(g, d).start()
        own[g] = pair_sum(g, x)

    def wgrad(g, carry):
        for pair in range(2):
            t = 4 * g + 2 * pair
            both = jnp.concatenate([g_window(t), g_window(t + 1)], axis=1)
            terms = jnp.dot(xt[...], both, preferred_element_type=F32)
            part[g, 2 * pair] = terms[:, :128].reshape(2, 4, 2, 16, 128)
            part[g, 2 * pair + 1] = terms[:, 128:].reshape(2, 4, 2, 16, 128)
        to_sibling(g).start()

        @pl.when(g > 0)
        def _():
            send_x(g - 1)

        return carry

    lax.fori_loop(0, GROUPS, wgrad, 0)
    loads[2].wait()
    send_x(GROUPS - 1)
    halo(xc, xface, xfr, 17, "recv")
    shift_all(xc, xfr, x3)
    acc_f[...] = jnp.zeros_like(acc_f)
    acc_b[...] = jnp.zeros_like(acc_b)

    def convolve(t0, count):
        for t in range(0, count, 2):
            n = min(2, count - t)
            wins = [g_window(t0 + t + i) for i in range(n)]
            kers = [wv[t0 + t + i] for i in range(n)]
            win = jnp.concatenate(wins, axis=1) if n == 2 else wins[0]
            ker = jnp.concatenate(kers, axis=1) if n == 2 else kers[0]
            acc_b[...] += lax.dot_general(win, ker, (((1,), (1,)), ((), ())), preferred_element_type=F32)
        for t in range(count):
            acc_f[...] += jnp.dot(x_window(t0 + t), wv[t0 + t], preferred_element_type=F32)

    def own_group():
        for slot in range(7):
            from_y(slot).wait_recv()
        total = own[y]
        for slot in range(7):
            total = total + decode(y_recv.at[slot], 8)
        total = total.reshape(4, 2, 16, 128)
        for h in range(2):
            encode(total[:, h], z_send.at[h])
        for d in range(1, 8):
            to_z(d).start()
        z_own[...] = jnp.where(zh == 0, total[:, 0], total[:, 1])

    def finish_group():
        for d in range(1, 8):
            to_z(d).wait_recv()
        total = z_own[...]
        for d in range(1, 8):
            total = total + decode(z_recv.at[d - 1], 4)
        kg[y] = total / jnp.sqrt(F32(131072))
        for d in range(1, 8):
            gather(d).start()

    def reduce(g, carry):
        for d in (1, 3, 2):
            to_x(g, d).wait_recv()
        total = own[g]
        for d in (1, 3, 2):
            total = total + decode(x_recv.at[g, d - 1], 8)

        @pl.when(y == g)
        def _():
            own[g] = total

        @pl.when(y != g)
        def _():
            encode(total, y_send.at[g])
            to_y(g).start()

        convolve(4 * g, 3)

        @pl.when(g < GROUPS - 1)
        def _():
            convolve(4 * g + 3, 1)

        @pl.when((g >= 2) & (y == g - 2))
        def _():
            own_group()

        @pl.when((g >= 4) & (y == g - 4))
        def _():
            finish_group()

        return carry

    lax.fori_loop(0, GROUPS, reduce, 0)
    out_v[...] = acc_f[...].astype(BF16).reshape(2, 8, 16, 128)
    back_v[...] = acc_b[...].astype(BF16).reshape(2, 8, 16, 256)
    stores = [
        pltpu.make_async_copy(out_v, out_hbm, out_sem.at[0]),
        pltpu.make_async_copy(back_v, back_hbm, out_sem.at[1]),
    ]
    for store in stores:
        store.start()

    @pl.when((y >= 5) & (y < GROUPS))
    def _():
        own_group()

    @pl.when((y >= 3) & (y < GROUPS))
    def _():
        finish_group()

    halo(gc, gface, gfr, 0, "send")
    halo(xc, xface, xfr, 17, "send")

    def sent(g, carry):
        to_sibling(g).wait_send()
        for d in (1, 2, 3):
            to_x(g, d).wait_send()

        @pl.when(y != g)
        def _():
            to_y(g).wait_send()

        return carry

    lax.fori_loop(0, GROUPS, sent, 0)

    @pl.when(y < GROUPS)
    def _():
        for d in range(1, 8):
            to_z(d).wait_send()
            gather(d).wait_send()

    def arrived(g, carry):
        @pl.when(y != g)
        def _():
            gathered(g).wait_recv()

        return carry

    lax.fori_loop(0, GROUPS, arrived, 0)
    last = pltpu.make_async_copy(kg, kg_hbm, out_sem.at[2])
    last.start()
    for store in stores:
        store.wait()
    last.wait()


def per_device(volumes, weights, out_grads):
    vm = pltpu.VMEM
    dma = pltpu.SemaphoreType.DMA
    any_space = pl.BlockSpec(memory_space=pl.ANY)
    out, back, kg = pl.pallas_call(
        kernel,
        out_shape=(
            jax.ShapeDtypeStruct((2, 8, 16, 128), BF16),
            jax.ShapeDtypeStruct((2, 8, 16, 256), BF16),
            jax.ShapeDtypeStruct((GROUPS, 4, 16, 128), F32),
        ),
        in_specs=[any_space] * 3,
        out_specs=(any_space,) * 3,
        scratch_shapes=[
            vm((27, 256, 128), BF16), vm((4, 10, 16, 256), BF16), vm((4, 10, 16, 128), BF16),
            vm((3, 4, 10, 16, 256), BF16), vm((3, 4, 10, 16, 128), BF16),
            vm((16, 256), BF16), vm((16, 128), BF16), vm((3, 3, 16, 256), BF16), vm((3, 3, 16, 128), BF16),
            vm((256, 256), BF16),
            vm((GROUPS, 4, 2, 4, 2, 16, 128), F32), vm((GROUPS, 4, 2, 4, 16, 128), F32),
            vm((GROUPS, 3, 9, 16, 128), BF16), vm((GROUPS, 3, 9, 16, 128), BF16),
            vm((GROUPS, 8, 16, 128), F32),
            vm((GROUPS, 9, 16, 128), BF16), vm((7, 9, 16, 128), BF16),
            vm((4, 16, 128), F32), vm((2, 5, 16, 128), BF16), vm((7, 5, 16, 128), BF16),
            vm((GROUPS, 4, 16, 128), F32),
            vm((256, 128), F32), vm((256, 256), F32),
            vm((2, 8, 16, 128), BF16), vm((2, 8, 16, 256), BF16),
            dma((3,)), dma((3,)), dma((34,)), dma((34,)), dma((GROUPS,)), dma((GROUPS,)),
            dma((GROUPS, 3)), dma((GROUPS, 3)), dma((GROUPS,)), dma((7,)), dma((7,)), dma((7,)),
            dma((7,)), dma((GROUPS,)),
        ],
        compiler_params=pltpu.CompilerParams(
            collective_id=0, has_side_effects=True, vmem_limit_bytes=60 * 2**20),
        cost_estimate=pl.CostEstimate(flops=1400000000, bytes_accessed=3000000, transcendentals=0),
    )(volumes.reshape(2, 8, 16, 256), weights.reshape(27, 256, 128), out_grads.reshape(2, 8, 16, 128))
    kg = kg.reshape(28, 16, 128)[:27].reshape(3, 3, 3, 16, 128)
    return out[None, None], back[None, None], kg


def solution(mesh):
    block = P("replica", "space", None, None, None, None)
    return jax.shard_map(
        per_device, mesh=mesh, in_specs=(block, P(), block),
        out_specs=(block, block, P(None, None, None, "replica", None)), check_vma=False)
```

```python
import jax
import jax.numpy as jnp
from jax import lax
from jax.experimental import pallas as pl
from jax.experimental.pallas import tpu as pltpu
from jax.sharding import PartitionSpec as P

MESH = pl.DeviceIdType.MESH
F32 = jnp.float32
BF16 = jnp.bfloat16
GROUPS = 7
FAR_FIRST = (4, 3, 5, 2, 6, 1, 7)
LIFT = 32768.0
PLANE = [(-1, -1), (-1, 1), (1, -1), (1, 1), (-1, 0), (1, 0), (0, -1), (0, 1), (0, 0)]


def encode(u, msg):
    n = u.shape[0]
    top = jnp.max(jnp.max(jnp.abs(u), axis=0), axis=0, keepdims=True)
    top = jnp.maximum(top, 1e-30).astype(BF16)
    v = u * (LIFT / top.astype(F32))
    v2 = v * v
    v4 = v2 * v2
    msg[pl.ds(0, n)] = ((v4 * v2) * (v * jnp.abs(v))).astype(BF16)
    msg[n] = jnp.broadcast_to(top.astype(F32), (16, 128)).astype(BF16)


def decode(msg, n):
    y = msg[pl.ds(0, n)].astype(F32)
    scale = msg[n].astype(F32) * (1.0 / LIFT)
    a = jnp.abs(y)
    t = lax.rsqrt(lax.rsqrt(a))
    u = jnp.where(a == 0.0, 0.0, t * lax.rsqrt(t))
    return jnp.where(y < 0.0, -u, u) * scale


def kernel(
    x_hbm, w_hbm, g_hbm, out_ref, back_ref, kg_ref,
    wv, xc, gc, x3, g3, xface, gface, xfr, gfr, xt,
    part, sib_recv, x_send, x_recv, own, y_send, y_recv, z_send, z_recv, done, acc_f, acc_b,
    in_sem, halo_s, halo_r, sib_s, sib_r, xs_s, xs_r, ys_s, ys_r, zs_s, zs_r, ag_s, ag_r,
):
    s = lax.axis_index("space")
    r = lax.axis_index("replica")
    y, zl = s // 4, s % 4
    zh, x, c = r // 8, (r // 2) % 4, r % 2
    gx, gy, gz = s // 8, (s // 2) % 4, s % 2

    loads = [
        pltpu.make_async_copy(g_hbm, gc.at[pl.ds(1, 2), pl.ds(1, 8)], in_sem.at[0]),
        pltpu.make_async_copy(x_hbm, xc.at[pl.ds(1, 2), pl.ds(1, 8)], in_sem.at[1]),
        pltpu.make_async_copy(w_hbm, wv, in_sem.at[2]),
    ]
    for load in loads:
        load.start()
    for field in (gc, xc):
        none = jnp.zeros((1, 10, 16, field.shape[3]), BF16)
        field[pl.ds(0, 1)] = none
        field[pl.ds(3, 1)] = none
        none = jnp.zeros((2, 1, 16, field.shape[3]), BF16)
        field[pl.ds(1, 2), pl.ds(0, 1)] = none
        field[pl.ds(1, 2), pl.ds(9, 1)] = none
    gfr[...] = jnp.zeros_like(gfr)
    xfr[...] = jnp.zeros_like(xfr)

    def inside(ox, oy):
        return (gx + ox >= 0) & (gx + ox <= 3) & (gy + oy >= 0) & (gy + oy <= 3)

    def at(ox, oy, other):
        return ((gx + ox) * 8 + (gy + oy) * 2 + (1 - gz if other else gz), r)

    z = zh * 4 + zl
    sibling = (s, r + 1 - 2 * c)
    x_peers = [(s, zh * 8 + ((x + d) % 4) * 2 + c) for d in (1, 2, 3)]
    y_peers = {d: (((y + d) % 8) * 4 + zl, r) for d in FAR_FIRST}

    def z_peer(d):
        z_to = (z + d) % 8
        return (y * 4 + z_to % 4, (z_to // 4) * 8 + x * 2 + c)

    z_peers = {d: z_peer(d) for d in FAR_FIRST}

    barrier = pltpu.get_barrier_semaphore()

    def greet(who):
        pl.semaphore_signal(barrier, inc=1, device_id=who, device_id_type=MESH)

    expected = 18
    for ox, oy in PLANE:
        here = inside(ox, oy)
        if (ox, oy) == (0, 0):
            greet(at(0, 0, True))
            expected = expected + 1
            continue

        @pl.when(here)
        def _(ox=ox, oy=oy):
            greet(at(ox, oy, False))
            greet(at(ox, oy, True))

        expected = expected + jnp.where(here, 2, 0)
    for who in x_peers + list(y_peers.values()) + list(z_peers.values()) + [sibling]:
        greet(who)

    def cut(o, size):
        return (pl.ds(0, size), pl.ds(1, size)) if o == 0 else (
            (pl.ds(size - 1, 1), pl.ds(0, 1)) if o == 1 else (pl.ds(0, 1), pl.ds(size + 1, 1)))

    def slab(source, field, k, ox, oy, base):
        (xs, xd), (ys, yd) = cut(ox, 2), cut(oy, 8)
        return pltpu.make_async_remote_copy(
            source.at[xs, ys], field.at[xd, yd], halo_s.at[base + k], halo_r.at[base + k],
            device_id=at(ox, oy, False), device_id_type=MESH)

    def face(source, field, k, ox, oy, base):
        return pltpu.make_async_remote_copy(
            source, field.at[1 - ox, 1 - oy], halo_s.at[base + 8 + k], halo_r.at[base + 8 + k],
            device_id=at(ox, oy, True), device_id_type=MESH)

    def halo(message, source, field, base, do):
        for k, (ox, oy) in enumerate(PLANE):
            here = inside(-ox, -oy) if do == "wait_recv" else inside(ox, oy)
            if (ox, oy) == (0, 0):
                if message is face:
                    getattr(message(source, field, k, ox, oy, base), do)()
                continue

            @pl.when(here)
            def _(k=k, ox=ox, oy=oy):
                getattr(message(source, field, k, ox, oy, base), do)()

    rows = lax.broadcasted_iota(jnp.int32, (16, 256), 0)
    cols = lax.broadcasted_iota(jnp.int32, (16, 256), 1)
    pick = jnp.where(cols == rows * 16 + jnp.where(gz == 0, 15, 0), 1.0, 0.0).astype(BF16)

    def interior(field):
        return field[pl.ds(1, 2), pl.ds(1, 8)].reshape(256, field.shape[3])

    pl.semaphore_wait(barrier, expected)
    halo(slab, g_hbm, gc, 0, "start")
    loads[0].wait()
    gface[...] = jnp.dot(pick, interior(gc), preferred_element_type=F32).astype(BF16)
    halo(face, gface, gfr, 0, "start")
    loads[1].wait()
    xface[...] = jnp.dot(pick, interior(xc), preferred_element_type=F32).astype(BF16)
    xt[...] = interior(xc).T

    def shift_all(field, received, shifted):
        ch = field.shape[3]
        shifted[1] = field[...]
        ri = lax.broadcasted_iota(jnp.int32, (160, 208), 0)
        ci = lax.broadcasted_iota(jnp.int32, (160, 208), 1)
        zi, yi = ri % 16, ri // 16
        for layer in range(4):
            ox = (0, 1, 1, 2)[layer]
            xrow = (8, 0, 8, 0)[layer]
            face_row = jnp.where(yi == 0, 160 + xrow + 7, jnp.where(yi == 9, 192 + xrow, 176 + xrow + yi - 1))
            low_col = jnp.where(zi > 0, ri - 1, jnp.where(gz == 1, face_row, -1))
            high_col = jnp.where(zi < 15, ri + 1, jnp.where(gz == 0, face_row, -1))
            low = jnp.where(ci == low_col, 1.0, 0.0).astype(BF16)
            high = jnp.where(ci == high_col, 1.0, 0.0).astype(BF16)
            cells = jnp.concatenate([field[layer].reshape(160, ch), received[ox].reshape(48, ch)], axis=0)
            shifted[0, layer] = jnp.dot(low, cells, preferred_element_type=F32).astype(BF16).reshape(10, 16, ch)
            shifted[2, layer] = jnp.dot(high, cells, preferred_element_type=F32).astype(BF16).reshape(10, 16, ch)

    def tap_of(t):
        t = jnp.minimum(t, 26)
        return t // 9, (t // 3) % 3, t % 3

    def g_window(t):
        dx, dy, dz = tap_of(t)
        return g3[2 - dz, pl.ds(2 - dx, 2), pl.ds(2 - dy, 8)].reshape(256, 128)

    def x_window(t):
        dx, dy, dz = tap_of(t)
        return x3[dz, pl.ds(dx, 2), pl.ds(dy, 8)].reshape(256, 256)

    halo(slab, g_hbm, gc, 0, "wait_recv")
    halo(face, gface, gfr, 0, "wait_recv")
    shift_all(gc, gfr, g3)
    halo(slab, x_hbm, xc, 17, "start")
    halo(face, xface, xfr, 17, "start")

    def to_sibling(g):
        return pltpu.make_async_remote_copy(
            part.at[g, :, :, :, 1 - c], sib_recv.at[g], sib_s.at[g], sib_r.at[g],
            device_id=sibling, device_id_type=MESH)

    def to_x(g, d):
        return pltpu.make_async_remote_copy(
            x_send.at[g, d - 1], x_recv.at[g, d - 1], xs_s.at[g, d - 1], xs_r.at[g, d - 1],
            device_id=x_peers[d - 1], device_id_type=MESH)

    def to_y(g):
        slot = (g - y + 8) % 8 - 1
        return pltpu.make_async_remote_copy(
            y_send.at[g], y_recv.at[slot], ys_s.at[g], ys_r.at[slot],
            device_id=(g * 4 + zl, r), device_id_type=MESH)

    def from_y(slot):
        return pltpu.make_async_remote_copy(
            y_send.at[0], y_recv.at[slot], ys_s.at[0], ys_r.at[slot],
            device_id=y_peers[1], device_id_type=MESH)

    def to_z(d):
        z_to = (z + d) % 8
        return pltpu.make_async_remote_copy(
            z_send.at[z_to // 4], z_recv.at[z], zs_s.at[d - 1], zs_r.at[z],
            device_id=z_peers[d], device_id_type=MESH)

    def from_z(d):
        z_from = (z + d) % 8
        return pltpu.make_async_remote_copy(
            z_send.at[0], z_recv.at[z_from], zs_s.at[0], zs_r.at[z_from],
            device_id=z_peers[d], device_id_type=MESH)

    def to_all(d):
        return pltpu.make_async_remote_copy(
            done.at[y], done.at[y], ag_s.at[d - 1], ag_r.at[y],
            device_id=y_peers[d], device_id_type=MESH)

    def from_owner(g):
        return pltpu.make_async_remote_copy(
            done.at[g], done.at[g], ag_s.at[0], ag_r.at[g],
            device_id=y_peers[1], device_id_type=MESH)

    def pair_sum(g, xx):
        mine = part[g, :, :, pl.ds(xx, 1), pl.ds(c, 1)].reshape(8, 16, 128)
        return mine + sib_recv[g, :, :, pl.ds(xx, 1)].reshape(8, 16, 128)

    def send_x(g):
        to_sibling(g).wait_recv()
        for d in (2, 1, 3):
            encode(pair_sum(g, (x + d) % 4), x_send.at[g, d - 1])
            to_x(g, d).start()
        own[g] = pair_sum(g, x)

    def wgrad(g, carry):
        for pair in range(2):
            t = 4 * g + 2 * pair
            both = jnp.concatenate([g_window(t), g_window(t + 1)], axis=1)
            terms = jnp.dot(xt[...], both, preferred_element_type=F32)
            part[g, 2 * pair] = terms[:, :128].reshape(2, 4, 2, 16, 128)
            part[g, 2 * pair + 1] = terms[:, 128:].reshape(2, 4, 2, 16, 128)
        to_sibling(g).start()

        @pl.when(g > 0)
        def _():
            send_x(g - 1)

        return carry

    lax.fori_loop(0, GROUPS, wgrad, 0)
    send_x(GROUPS - 1)
    loads[2].wait()
    acc_b[...] = jnp.zeros_like(acc_b)
    acc_f[...] = jnp.zeros_like(acc_f)

    def backward(t0, count):
        for t in range(0, count, 2):
            n = min(2, count - t)
            wins = [g_window(t0 + t + i) for i in range(n)]
            kers = [wv[t0 + t + i] for i in range(n)]
            win = jnp.concatenate(wins, axis=1) if n == 2 else wins[0]
            ker = jnp.concatenate(kers, axis=1) if n == 2 else kers[0]
            acc_b[...] += lax.dot_general(win, ker, (((1,), (1,)), ((), ())), preferred_element_type=F32)

    def reduce(g, carry):
        for d in (1, 3, 2):
            to_x(g, d).wait_recv()
        total = own[g]
        for d in (1, 3, 2):
            total = total + decode(x_recv.at[g, d - 1], 8)

        @pl.when(y == g)
        def _():
            own[g] = total

        @pl.when(y != g)
        def _():
            encode(total, y_send.at[g])
            to_y(g).start()

        backward(4 * g, 3)

        @pl.when(g < GROUPS - 1)
        def _():
            backward(4 * g + 3, 1)

        return carry

    lax.fori_loop(0, GROUPS, reduce, 0)

    halo(slab, x_hbm, xc, 17, "wait_recv")
    halo(face, xface, xfr, 17, "wait_recv")
    shift_all(xc, xfr, x3)

    def forward(k, carry):
        for i in range(3):
            acc_f[...] += jnp.dot(x_window(3 * k + i), wv[3 * k + i], preferred_element_type=F32)
        return carry

    lax.fori_loop(0, 9, forward, 0)

    @pl.when(y < GROUPS)
    def _():
        for slot in range(7):
            from_y(slot).wait_recv()
        total = own[y]
        for slot in range(7):
            total = total + decode(y_recv.at[slot], 8)
        total = total.reshape(4, 2, 16, 128)
        for h in range(2):
            encode(total[:, h], z_send.at[h])
        for d in FAR_FIRST:
            to_z(d).start()
        z_recv[z] = z_send[zh]

    back_ref[...] = acc_b[...].astype(BF16).reshape(2, 8, 16, 256)
    out_ref[...] = acc_f[...].astype(BF16).reshape(2, 8, 16, 128)

    def sent(g, carry):
        to_sibling(g).wait_send()
        for d in (1, 2, 3):
            to_x(g, d).wait_send()

        @pl.when(y != g)
        def _():
            to_y(g).wait_send()

        return carry

    lax.fori_loop(0, GROUPS, sent, 0)
    for source, field, base in ((g_hbm, gc, 0), (x_hbm, xc, 17)):
        halo(slab, source, field, base, "wait_send")
    for source, field, base in ((gface, gfr, 0), (xface, xfr, 17)):
        halo(face, source, field, base, "wait_send")

    @pl.when(y < GROUPS)
    def _():
        for d in FAR_FIRST:
            from_z(d).wait_recv()
        total = decode(z_recv.at[0], 4)
        for k in range(1, 8):
            total = total + decode(z_recv.at[k], 4)
        encode(total / jnp.sqrt(F32(131072)), done.at[y])
        for d in FAR_FIRST:
            to_all(d).start()
        for d in FAR_FIRST:
            to_z(d).wait_send()

    def arrived(g, carry):
        @pl.when(y != g)
        def _():
            from_owner(g).wait_recv()

        kg_ref[g] = decode(done.at[g], 4)
        return carry

    lax.fori_loop(0, GROUPS, arrived, 0)

    @pl.when(y < GROUPS)
    def _():
        for d in FAR_FIRST:
            to_all(d).wait_send()


def per_device(volumes, weights, out_grads):
    vm = pltpu.VMEM
    dma = pltpu.SemaphoreType.DMA
    in_hbm = pl.BlockSpec(memory_space=pltpu.HBM)
    in_vmem = pl.BlockSpec(memory_space=pltpu.VMEM)
    out, back, kg = pl.pallas_call(
        kernel,
        out_shape=(
            jax.ShapeDtypeStruct((2, 8, 16, 128), BF16),
            jax.ShapeDtypeStruct((2, 8, 16, 256), BF16),
            jax.ShapeDtypeStruct((GROUPS, 4, 16, 128), F32),
        ),
        in_specs=[in_hbm] * 3,
        out_specs=(in_vmem,) * 3,
        scratch_shapes=[
            vm((27, 256, 128), BF16), vm((4, 10, 16, 256), BF16), vm((4, 10, 16, 128), BF16),
            vm((3, 4, 10, 16, 256), BF16), vm((3, 4, 10, 16, 128), BF16),
            vm((16, 256), BF16), vm((16, 128), BF16), vm((3, 3, 16, 256), BF16), vm((3, 3, 16, 128), BF16),
            vm((256, 256), BF16),
            vm((GROUPS, 4, 2, 4, 2, 16, 128), F32), vm((GROUPS, 4, 2, 4, 16, 128), F32),
            vm((GROUPS, 3, 9, 16, 128), BF16), vm((GROUPS, 3, 9, 16, 128), BF16),
            vm((GROUPS, 8, 16, 128), F32),
            vm((GROUPS, 9, 16, 128), BF16), vm((7, 9, 16, 128), BF16),
            vm((2, 5, 16, 128), BF16), vm((8, 5, 16, 128), BF16), vm((GROUPS, 5, 16, 128), BF16),
            vm((256, 128), F32), vm((256, 256), F32),
            dma((3,)), dma((34,)), dma((34,)), dma((GROUPS,)), dma((GROUPS,)),
            dma((GROUPS, 3)), dma((GROUPS, 3)), dma((GROUPS,)), dma((7,)), dma((7,)), dma((8,)),
            dma((7,)), dma((GROUPS,)),
        ],
        compiler_params=pltpu.CompilerParams(
            collective_id=0, has_side_effects=True, vmem_limit_bytes=53 * 2**20),
        cost_estimate=pl.CostEstimate(flops=1400000000, bytes_accessed=3000000, transcendentals=0),
    )(volumes.reshape(2, 8, 16, 256), weights.reshape(27, 256, 128), out_grads.reshape(2, 8, 16, 128))
    kg = kg.reshape(28, 16, 128)[:27].reshape(3, 3, 3, 16, 128)
    return out[None, None], back[None, None], kg


def solution(mesh):
    block = P("replica", "space", None, None, None, None)
    return jax.shard_map(
        per_device, mesh=mesh, in_specs=(block, P(), block),
        out_specs=(block, block, P(None, None, None, "replica", None)), check_vma=False)
```

```python
import jax
import jax.numpy as jnp
from jax import lax
from jax.experimental import pallas as pl
from jax.experimental.pallas import tpu as pltpu
from jax.sharding import PartitionSpec as P

MESH = pl.DeviceIdType.MESH
F32 = jnp.float32
BF16 = jnp.bfloat16
GROUPS = 7
FAR_FIRST = (4, 3, 5, 2, 6, 1, 7)
LIFT = 32768.0
PLANE = [(-1, -1), (-1, 1), (1, -1), (1, 1), (-1, 0), (1, 0), (0, -1), (0, 1), (0, 0)]


def encode(u, msg):
    n = u.shape[0]
    top = jnp.max(jnp.max(jnp.abs(u), axis=0), axis=0, keepdims=True)
    top = jnp.maximum(top, 1e-30).astype(BF16)
    v = u * (LIFT / top.astype(F32))
    v2 = v * v
    v4 = v2 * v2
    msg[pl.ds(0, n)] = ((v4 * v2) * (v * jnp.abs(v))).astype(BF16)
    msg[n] = jnp.broadcast_to(top.astype(F32), (16, 128)).astype(BF16)


def decode(msg, n):
    y = msg[pl.ds(0, n)].astype(F32)
    scale = msg[n].astype(F32) * (1.0 / LIFT)
    a = jnp.abs(y)
    t = lax.rsqrt(lax.rsqrt(a))
    u = jnp.where(a == 0.0, 0.0, t * lax.rsqrt(t))
    return jnp.where(y < 0.0, -u, u) * scale


def kernel(
    x_hbm, w_hbm, g_hbm, out_ref, back_ref, kg_ref,
    wv, xc, gc, gc2, x3, g3, g32, xface, gface, xfr, gfr, gfr2, xt, xt2,
    part_a, part_b, x_send, x_recv, own_a, y_send, y_recv, b_send, b_recv, bx_send, bx_recv,
    z_send, z_recv, done, acc_f, acc_b,
    in_sem, halo_s, halo_r, sib_s, sib_r, xs_s, xs_r, ys_s, ys_r, bs_s, bs_r, bx_s, bx_r, zs_s, zs_r, ag_s, ag_r,
):
    s = lax.axis_index("space")
    r = lax.axis_index("replica")
    y, zl = s // 4, s % 4
    zh, x, c = r // 8, (r // 2) % 4, r % 2
    gx, gy, gz = s // 8, (s // 2) % 4, s % 2

    loads = [
        pltpu.make_async_copy(g_hbm, gc.at[pl.ds(1, 2), pl.ds(1, 8)], in_sem.at[0]),
        pltpu.make_async_copy(x_hbm, xc.at[pl.ds(1, 2), pl.ds(1, 8)], in_sem.at[1]),
        pltpu.make_async_copy(w_hbm, wv, in_sem.at[2]),
    ]
    for load in loads:
        load.start()
    for field in (gc, xc):
        none = jnp.zeros((1, 10, 16, field.shape[3]), BF16)
        field[pl.ds(0, 1)] = none
        field[pl.ds(3, 1)] = none
        none = jnp.zeros((2, 1, 16, field.shape[3]), BF16)
        field[pl.ds(1, 2), pl.ds(0, 1)] = none
        field[pl.ds(1, 2), pl.ds(9, 1)] = none
    gfr[...] = jnp.zeros_like(gfr)
    xfr[...] = jnp.zeros_like(xfr)

    def inside(ox, oy):
        return (gx + ox >= 0) & (gx + ox <= 3) & (gy + oy >= 0) & (gy + oy <= 3)

    def at(ox, oy, other):
        return ((gx + ox) * 8 + (gy + oy) * 2 + (1 - gz if other else gz), r)

    z = zh * 4 + zl
    sibling = (s, r + 1 - 2 * c)
    x_peers = [(s, zh * 8 + ((x + d) % 4) * 2 + c) for d in (1, 2, 3)]
    y_peers = {d: (((y + d) % 8) * 4 + zl, r) for d in FAR_FIRST}

    def z_peer(d):
        z_to = (z + d) % 8
        return (y * 4 + z_to % 4, (z_to // 4) * 8 + x * 2 + c)

    z_peers = {d: z_peer(d) for d in FAR_FIRST}

    barrier = pltpu.get_barrier_semaphore()

    def greet(who):
        pl.semaphore_signal(barrier, inc=1, device_id=who, device_id_type=MESH)

    expected = 18
    for ox, oy in PLANE:
        here = inside(ox, oy)
        if (ox, oy) == (0, 0):
            greet(at(0, 0, True))
            expected = expected + 1
            continue

        @pl.when(here)
        def _(ox=ox, oy=oy):
            greet(at(ox, oy, False))
            greet(at(ox, oy, True))

        expected = expected + jnp.where(here, 2, 0)
    for who in x_peers + list(y_peers.values()) + list(z_peers.values()) + [sibling]:
        greet(who)

    def cut(o, size):
        return (pl.ds(0, size), pl.ds(1, size)) if o == 0 else (
            (pl.ds(size - 1, 1), pl.ds(0, 1)) if o == 1 else (pl.ds(0, 1), pl.ds(size + 1, 1)))

    def slab(source, field, k, ox, oy, base):
        (xs, xd), (ys, yd) = cut(ox, 2), cut(oy, 8)
        return pltpu.make_async_remote_copy(
            source.at[xs, ys], field.at[xd, yd], halo_s.at[base + k], halo_r.at[base + k],
            device_id=at(ox, oy, False), device_id_type=MESH)

    def face(source, field, k, ox, oy, base):
        return pltpu.make_async_remote_copy(
            source, field.at[1 - ox, 1 - oy], halo_s.at[base + 8 + k], halo_r.at[base + 8 + k],
            device_id=at(ox, oy, True), device_id_type=MESH)

    def halo(message, source, field, base, do):
        for k, (ox, oy) in enumerate(PLANE):
            here = inside(-ox, -oy) if do == "wait_recv" else inside(ox, oy)
            if (ox, oy) == (0, 0):
                if message is face:
                    getattr(message(source, field, k, ox, oy, base), do)()
                continue

            @pl.when(here)
            def _(k=k, ox=ox, oy=oy):
                getattr(message(source, field, k, ox, oy, base), do)()

    def share(k):
        source, target = ((xt.at[:, 1 - c], xt2), (gc, gc2), (gfr, gfr2))[k]
        return pltpu.make_async_remote_copy(
            source, target, sib_s.at[k], sib_r.at[k], device_id=sibling, device_id_type=MESH)

    rows = lax.broadcasted_iota(jnp.int32, (16, 256), 0)
    cols = lax.broadcasted_iota(jnp.int32, (16, 256), 1)
    pick = jnp.where(cols == rows * 16 + jnp.where(gz == 0, 15, 0), 1.0, 0.0).astype(BF16)

    def interior(field):
        return field[pl.ds(1, 2), pl.ds(1, 8)].reshape(256, field.shape[3])

    pl.semaphore_wait(barrier, expected)
    halo(slab, g_hbm, gc, 0, "start")
    loads[0].wait()
    gface[...] = jnp.dot(pick, interior(gc), preferred_element_type=F32).astype(BF16)
    halo(face, gface, gfr, 0, "start")
    loads[1].wait()
    xface[...] = jnp.dot(pick, interior(xc), preferred_element_type=F32).astype(BF16)
    xt[...] = interior(xc).T.reshape(8, 2, 16, 256)
    share(0).start()

    def shift_all(field, received, shifted):
        ch = field.shape[3]
        shifted[1] = field[...]
        ri = lax.broadcasted_iota(jnp.int32, (160, 208), 0)
        ci = lax.broadcasted_iota(jnp.int32, (160, 208), 1)
        zi, yi = ri % 16, ri // 16
        for layer in range(4):
            ox = (0, 1, 1, 2)[layer]
            xrow = (8, 0, 8, 0)[layer]
            face_row = jnp.where(yi == 0, 160 + xrow + 7, jnp.where(yi == 9, 192 + xrow, 176 + xrow + yi - 1))
            low_col = jnp.where(zi > 0, ri - 1, jnp.where(gz == 1, face_row, -1))
            high_col = jnp.where(zi < 15, ri + 1, jnp.where(gz == 0, face_row, -1))
            low = jnp.where(ci == low_col, 1.0, 0.0).astype(BF16)
            high = jnp.where(ci == high_col, 1.0, 0.0).astype(BF16)
            cells = jnp.concatenate([field[layer].reshape(160, ch), received[ox].reshape(48, ch)], axis=0)
            shifted[0, layer] = jnp.dot(low, cells, preferred_element_type=F32).astype(BF16).reshape(10, 16, ch)
            shifted[2, layer] = jnp.dot(high, cells, preferred_element_type=F32).astype(BF16).reshape(10, 16, ch)

    def tap_of(t):
        t = jnp.minimum(t, 26)
        return t // 9, (t // 3) % 3, t % 3

    def g_window(t, field):
        dx, dy, dz = tap_of(t)
        return field[2 - dz, pl.ds(2 - dx, 2), pl.ds(2 - dy, 8)].reshape(256, 128)

    def x_window(t):
        dx, dy, dz = tap_of(t)
        return x3[dz, pl.ds(dx, 2), pl.ds(dy, 8)].reshape(256, 256)

    halo(slab, g_hbm, gc, 0, "wait_recv")
    halo(face, gface, gfr, 0, "wait_recv")
    share(1).start()
    share(2).start()
    shift_all(gc, gfr, g3)
    halo(slab, x_hbm, xc, 17, "start")
    halo(face, xface, xfr, 17, "start")
    for k in (1, 2, 0):
        share(k).wait_recv()
    shift_all(gc2, gfr2, g32)

    def to_x(g, d):
        return pltpu.make_async_remote_copy(
            x_send.at[g, d - 1], x_recv.at[g, d - 1], xs_s.at[g, d - 1], xs_r.at[g, d - 1],
            device_id=x_peers[d - 1], device_id_type=MESH)

    def to_b(d):
        return pltpu.make_async_remote_copy(
            b_send.at[d - 1], b_recv.at[d - 1], bs_s.at[d - 1], bs_r.at[d - 1],
            device_id=(((y + d) % 8) * 4 + zl, r), device_id_type=MESH)

    def to_bx(d):
        return pltpu.make_async_remote_copy(
            bx_send.at[d - 1], bx_recv.at[d - 1], bx_s.at[d - 1], bx_r.at[d - 1],
            device_id=x_peers[d - 1], device_id_type=MESH)

    def to_y(g):
        slot = (g - y + 8) % 8 - 1
        return pltpu.make_async_remote_copy(
            y_send.at[g], y_recv.at[slot], ys_s.at[g], ys_r.at[slot],
            device_id=(g * 4 + zl, r), device_id_type=MESH)

    def from_y(slot):
        return pltpu.make_async_remote_copy(
            y_send.at[0], y_recv.at[slot], ys_s.at[0], ys_r.at[slot],
            device_id=y_peers[1], device_id_type=MESH)

    def to_z(d):
        z_to = (z + d) % 8
        return pltpu.make_async_remote_copy(
            z_send.at[z_to // 4], z_recv.at[z], zs_s.at[d - 1], zs_r.at[z],
            device_id=z_peers[d], device_id_type=MESH)

    def from_z(d):
        z_from = (z + d) % 8
        return pltpu.make_async_remote_copy(
            z_send.at[0], z_recv.at[z_from], zs_s.at[0], zs_r.at[z_from],
            device_id=z_peers[d], device_id_type=MESH)

    def to_all(d):
        return pltpu.make_async_remote_copy(
            done.at[y], done.at[y], ag_s.at[d - 1], ag_r.at[y],
            device_id=y_peers[d], device_id_type=MESH)

    def from_owner(g):
        return pltpu.make_async_remote_copy(
            done.at[g], done.at[g], ag_s.at[0], ag_r.at[g],
            device_id=y_peers[1], device_id_type=MESH)

    def products(t):
        terms = jnp.zeros((128, 256), F32)
        for field, chans in ((g3, xt[:, c]), (g32, xt2[...])):
            both = jnp.concatenate([g_window(t, field), g_window(t + 1, field)], axis=1)
            terms = terms + jnp.dot(chans.reshape(128, 256), both, preferred_element_type=F32)
        return [terms[:, 128 * i : 128 * i + 128].reshape(2, 4, 16, 128) for i in range(2)]

    def step(i):
        dy = 4 + ((i + 1) // 2) * (1 - 2 * (i % 2))
        return dy, (y + dy) % 8

    def wgrad(i, carry):
        dy, q = step(i)

        @pl.when(q < GROUPS)
        def _():
            part_a[q, 2], part_b[...] = products(4 * q + 2)

            @pl.when(dy != 0)
            def _():
                encode(part_b[...].reshape(8, 16, 128), b_send.at[dy - 1])
                to_b(dy).start()

            part_a[q, 0], part_a[q, 1] = products(4 * q)
            for d in (2, 1, 3):
                encode(part_a[q, :, :, (x + d) % 4].reshape(6, 16, 128), x_send.at[q, d - 1])
                to_x(q, d).start()

        return carry

    lax.fori_loop(0, 8, wgrad, 0)
    loads[2].wait()
    acc_b[...] = jnp.zeros_like(acc_b)
    acc_f[...] = jnp.zeros_like(acc_f)

    def backward(t0, count):
        for t in range(0, count, 2):
            n = min(2, count - t)
            wins = [g_window(t0 + t + i, g3) for i in range(n)]
            kers = [wv[t0 + t + i] for i in range(n)]
            win = jnp.concatenate(wins, axis=1) if n == 2 else wins[0]
            ker = jnp.concatenate(kers, axis=1) if n == 2 else kers[0]
            acc_b[...] += lax.dot_general(win, ker, (((1,), (1,)), ((), ())), preferred_element_type=F32)

    def reduce(i, carry):
        dy, q = step(i)

        @pl.when(q < GROUPS)
        def _():
            for d in (1, 3, 2):
                to_x(q, d).wait_recv()
            total = part_a[q, :, :, x].reshape(6, 16, 128)
            for d in (1, 3, 2):
                total = total + decode(x_recv.at[q, d - 1], 6)

            @pl.when(dy == 0)
            def _():
                own_a[...] = total

            @pl.when(dy != 0)
            def _():
                encode(total, y_send.at[q])
                to_y(q).start()

        @pl.when(i < GROUPS)
        def _():
            backward(4 * i, 3)

        @pl.when(i < GROUPS - 1)
        def _():
            backward(4 * i + 3, 1)

        return carry

    lax.fori_loop(0, 8, reduce, 0)

    @pl.when(y < GROUPS)
    def _():
        for d in range(1, 8):
            to_b(d).wait_recv()
        total = part_b[...].reshape(8, 16, 128)
        for d in range(1, 8):
            total = total + decode(b_recv.at[d - 1], 8)
        part_b[...] = total.reshape(2, 4, 16, 128)
        for d in (2, 1, 3):
            encode(part_b[:, (x + d) % 4], bx_send.at[d - 1])
            to_bx(d).start()

    halo(slab, x_hbm, xc, 17, "wait_recv")
    halo(face, xface, xfr, 17, "wait_recv")
    shift_all(xc, xfr, x3)

    def forward(k, carry):
        for i in range(3):
            acc_f[...] += jnp.dot(x_window(3 * k + i), wv[3 * k + i], preferred_element_type=F32)
        return carry

    lax.fori_loop(0, 9, forward, 0)

    @pl.when(y < GROUPS)
    def _():
        for slot in range(7):
            from_y(slot).wait_recv()
        first = own_a[...]
        for slot in range(7):
            first = first + decode(y_recv.at[slot], 6)
        second = part_b[:, x]
        for d in (1, 2, 3):
            to_bx(d).wait_recv()
            second = second + decode(bx_recv.at[d - 1], 2)
        total = jnp.concatenate([first, second], axis=0).reshape(4, 2, 16, 128)
        for h in range(2):
            encode(total[:, h], z_send.at[h])
        for d in FAR_FIRST:
            to_z(d).start()
        z_recv[z] = z_send[zh]

    back_ref[...] = acc_b[...].astype(BF16).reshape(2, 8, 16, 256)
    out_ref[...] = acc_f[...].astype(BF16).reshape(2, 8, 16, 128)

    def sent(g, carry):
        for d in (1, 2, 3):
            to_x(g, d).wait_send()

        @pl.when(y != g)
        def _():
            to_y(g).wait_send()

        return carry

    lax.fori_loop(0, GROUPS, sent, 0)
    for k in range(3):
        share(k).wait_send()
    for d in range(1, 8):
        @pl.when((y + d) % 8 < GROUPS)
        def _(d=d):
            to_b(d).wait_send()
    for source, field, base in ((g_hbm, gc, 0), (x_hbm, xc, 17)):
        halo(slab, source, field, base, "wait_send")
    for source, field, base in ((gface, gfr, 0), (xface, xfr, 17)):
        halo(face, source, field, base, "wait_send")

    @pl.when(y < GROUPS)
    def _():
        for d in FAR_FIRST:
            from_z(d).wait_recv()
        total = decode(z_recv.at[0], 4)
        for k in range(1, 8):
            total = total + decode(z_recv.at[k], 4)
        encode(total / jnp.sqrt(F32(131072)), done.at[y])
        for d in FAR_FIRST:
            to_all(d).start()
        for d in FAR_FIRST:
            to_z(d).wait_send()
        for d in (1, 2, 3):
            to_bx(d).wait_send()

    def arrived(g, carry):
        @pl.when(y != g)
        def _():
            from_owner(g).wait_recv()

        kg_ref[g] = decode(done.at[g], 4)
        return carry

    lax.fori_loop(0, GROUPS, arrived, 0)

    @pl.when(y < GROUPS)
    def _():
        for d in FAR_FIRST:
            to_all(d).wait_send()


def per_device(volumes, weights, out_grads):
    vm = pltpu.VMEM
    dma = pltpu.SemaphoreType.DMA
    in_hbm = pl.BlockSpec(memory_space=pltpu.HBM)
    in_vmem = pl.BlockSpec(memory_space=pltpu.VMEM)
    out, back, kg = pl.pallas_call(
        kernel,
        out_shape=(
            jax.ShapeDtypeStruct((2, 8, 16, 128), BF16),
            jax.ShapeDtypeStruct((2, 8, 16, 256), BF16),
            jax.ShapeDtypeStruct((GROUPS, 4, 16, 128), F32),
        ),
        in_specs=[in_hbm] * 3,
        out_specs=(in_vmem,) * 3,
        scratch_shapes=[
            vm((27, 256, 128), BF16), vm((4, 10, 16, 256), BF16), vm((4, 10, 16, 128), BF16), vm((4, 10, 16, 128), BF16),
            vm((3, 4, 10, 16, 256), BF16), vm((3, 4, 10, 16, 128), BF16), vm((3, 4, 10, 16, 128), BF16),
            vm((16, 256), BF16), vm((16, 128), BF16), vm((3, 3, 16, 256), BF16), vm((3, 3, 16, 128), BF16),
            vm((3, 3, 16, 128), BF16), vm((8, 2, 16, 256), BF16), vm((8, 16, 256), BF16),
            vm((GROUPS, 3, 2, 4, 16, 128), F32), vm((2, 4, 16, 128), F32),
            vm((GROUPS, 3, 7, 16, 128), BF16), vm((GROUPS, 3, 7, 16, 128), BF16), vm((6, 16, 128), F32),
            vm((GROUPS, 7, 16, 128), BF16), vm((7, 7, 16, 128), BF16),
            vm((7, 9, 16, 128), BF16), vm((7, 9, 16, 128), BF16),
            vm((3, 3, 16, 128), BF16), vm((3, 3, 16, 128), BF16),
            vm((2, 5, 16, 128), BF16), vm((8, 5, 16, 128), BF16), vm((GROUPS, 5, 16, 128), BF16),
            vm((256, 128), F32), vm((256, 256), F32),
            dma((3,)), dma((34,)), dma((34,)), dma((3,)), dma((3,)),
            dma((GROUPS, 3)), dma((GROUPS, 3)), dma((GROUPS,)), dma((7,)),
            dma((7,)), dma((7,)), dma((3,)), dma((3,)), dma((7,)), dma((8,)),
            dma((7,)), dma((GROUPS,)),
        ],
        compiler_params=pltpu.CompilerParams(
            collective_id=0, has_side_effects=True, vmem_limit_bytes=53 * 2**20),
        cost_estimate=pl.CostEstimate(flops=1400000000, bytes_accessed=3000000, transcendentals=0),
    )(volumes.reshape(2, 8, 16, 256), weights.reshape(27, 256, 128), out_grads.reshape(2, 8, 16, 128))
    kg = kg.reshape(28, 16, 128)[:27].reshape(3, 3, 3, 16, 128)
    return out[None, None], back[None, None], kg


def solution(mesh):
    block = P("replica", "space", None, None, None, None)
    return jax.shard_map(
        per_device, mesh=mesh, in_specs=(block, P(), block),
        out_specs=(block, block, P(None, None, None, "replica", None)), check_vma=False)
```

```python
import jax
import jax.numpy as jnp
from jax import lax
from jax.experimental import pallas as pl
from jax.experimental.pallas import tpu as pltpu
from jax.sharding import PartitionSpec as P

MESH = pl.DeviceIdType.MESH
F32 = jnp.float32
BF16 = jnp.bfloat16
GROUPS = 7
FAR_FIRST = (4, 3, 5, 2, 6, 1, 7)
LIFT = 32768.0
PLANE = [(-1, -1), (-1, 1), (1, -1), (1, 1), (-1, 0), (1, 0), (0, -1), (0, 1), (0, 0)]


def encode(u, msg):
    n = u.shape[0]
    top = jnp.max(jnp.max(jnp.abs(u), axis=0), axis=0, keepdims=True)
    top = jnp.maximum(top, 1e-30).astype(BF16)
    v = u * (LIFT / top.astype(F32))
    v2 = v * v
    v4 = v2 * v2
    msg[pl.ds(0, n)] = ((v4 * v2) * (v * jnp.abs(v))).astype(BF16)
    msg[n] = jnp.broadcast_to(top.astype(F32), (16, 128)).astype(BF16)


def decode(msg, n):
    y = msg[pl.ds(0, n)].astype(F32)
    scale = msg[n].astype(F32) * (1.0 / LIFT)
    a = jnp.abs(y)
    t = lax.rsqrt(lax.rsqrt(a))
    u = jnp.where(a == 0.0, 0.0, t * lax.rsqrt(t))
    return jnp.where(y < 0.0, -u, u) * scale


def kernel(
    x_hbm, w_hbm, g_hbm, out_ref, back_ref, kg_ref,
    wv, xc, gc, gc2, x3, g3, g32, xface, gface, xfr, gfr, gfr2, xt, xt2,
    part_a, part_b, x_send, x_recv, own_a, y_send, y_recv, b_send, b_recv, bx_send, bx_recv,
    z_send, z_recv, done, acc_f, acc_b,
    in_sem, halo_s, halo_r, sib_s, sib_r, xs_s, xs_r, ys_s, ys_r, bs_s, bs_r, bx_s, bx_r, zs_s, zs_r, ag_s, ag_r,
):
    s = lax.axis_index("space")
    r = lax.axis_index("replica")
    y, zl = s // 4, s % 4
    zh, x, c = r // 8, (r // 2) % 4, r % 2
    gx, gy, gz = s // 8, (s // 2) % 4, s % 2

    loads = [
        pltpu.make_async_copy(g_hbm, gc.at[pl.ds(1, 2), pl.ds(1, 8)], in_sem.at[0]),
        pltpu.make_async_copy(x_hbm, xc.at[pl.ds(1, 2), pl.ds(1, 8)], in_sem.at[1]),
        pltpu.make_async_copy(w_hbm, wv, in_sem.at[2]),
    ]
    for load in loads:
        load.start()
    for field in (gc, xc):
        none = jnp.zeros((1, 10, 16, field.shape[3]), BF16)
        field[pl.ds(0, 1)] = none
        field[pl.ds(3, 1)] = none
        none = jnp.zeros((2, 1, 16, field.shape[3]), BF16)
        field[pl.ds(1, 2), pl.ds(0, 1)] = none
        field[pl.ds(1, 2), pl.ds(9, 1)] = none
    gfr[...] = jnp.zeros_like(gfr)
    xfr[...] = jnp.zeros_like(xfr)

    def inside(ox, oy):
        return (gx + ox >= 0) & (gx + ox <= 3) & (gy + oy >= 0) & (gy + oy <= 3)

    def at(ox, oy, other):
        return ((gx + ox) * 8 + (gy + oy) * 2 + (1 - gz if other else gz), r)

    z = zh * 4 + zl
    sibling = (s, r + 1 - 2 * c)
    x_peers = [(s, zh * 8 + ((x + d) % 4) * 2 + c) for d in (1, 2, 3)]
    y_peers = {d: (((y + d) % 8) * 4 + zl, r) for d in FAR_FIRST}

    def z_peer(d):
        z_to = (z + d) % 8
        return (y * 4 + z_to % 4, (z_to // 4) * 8 + x * 2 + c)

    z_peers = {d: z_peer(d) for d in FAR_FIRST}

    barrier = pltpu.get_barrier_semaphore()

    def greet(who):
        pl.semaphore_signal(barrier, inc=1, device_id=who, device_id_type=MESH)

    expected = 18
    for ox, oy in PLANE:
        here = inside(ox, oy)
        if (ox, oy) == (0, 0):
            greet(at(0, 0, True))
            expected = expected + 1
            continue

        @pl.when(here)
        def _(ox=ox, oy=oy):
            greet(at(ox, oy, False))
            greet(at(ox, oy, True))

        expected = expected + jnp.where(here, 2, 0)
    for who in x_peers + list(y_peers.values()) + list(z_peers.values()) + [sibling]:
        greet(who)

    def cut(o, size):
        return (pl.ds(0, size), pl.ds(1, size)) if o == 0 else (
            (pl.ds(size - 1, 1), pl.ds(0, 1)) if o == 1 else (pl.ds(0, 1), pl.ds(size + 1, 1)))

    def slab(source, field, k, ox, oy, base):
        (xs, xd), (ys, yd) = cut(ox, 2), cut(oy, 8)
        return pltpu.make_async_remote_copy(
            source.at[xs, ys], field.at[xd, yd], halo_s.at[base + k], halo_r.at[base + k],
            device_id=at(ox, oy, False), device_id_type=MESH)

    def face(source, field, k, ox, oy, base):
        return pltpu.make_async_remote_copy(
            source, field.at[1 - ox, 1 - oy], halo_s.at[base + 8 + k], halo_r.at[base + 8 + k],
            device_id=at(ox, oy, True), device_id_type=MESH)

    def halo(message, source, field, base, do):
        for k, (ox, oy) in enumerate(PLANE):
            here = inside(-ox, -oy) if do == "wait_recv" else inside(ox, oy)
            if (ox, oy) == (0, 0):
                if message is face:
                    getattr(message(source, field, k, ox, oy, base), do)()
                continue

            @pl.when(here)
            def _(k=k, ox=ox, oy=oy):
                getattr(message(source, field, k, ox, oy, base), do)()

    def share(k):
        source, target = ((xt.at[:, 1 - c], xt2), (gc, gc2), (gfr, gfr2))[k]
        return pltpu.make_async_remote_copy(
            source, target, sib_s.at[k], sib_r.at[k], device_id=sibling, device_id_type=MESH)

    rows = lax.broadcasted_iota(jnp.int32, (16, 256), 0)
    cols = lax.broadcasted_iota(jnp.int32, (16, 256), 1)
    pick = jnp.where(cols == rows * 16 + jnp.where(gz == 0, 15, 0), 1.0, 0.0).astype(BF16)

    def interior(field):
        return field[pl.ds(1, 2), pl.ds(1, 8)].reshape(256, field.shape[3])

    pl.semaphore_wait(barrier, expected)
    halo(slab, g_hbm, gc, 0, "start")
    loads[0].wait()
    gface[...] = jnp.dot(pick, interior(gc), preferred_element_type=F32).astype(BF16)
    halo(face, gface, gfr, 0, "start")
    loads[1].wait()
    xface[...] = jnp.dot(pick, interior(xc), preferred_element_type=F32).astype(BF16)
    xt[...] = interior(xc).T.reshape(8, 2, 16, 256)
    share(0).start()

    def shift_all(field, received, shifted):
        ch = field.shape[3]
        shifted[1] = field[...]
        ri = lax.broadcasted_iota(jnp.int32, (160, 208), 0)
        ci = lax.broadcasted_iota(jnp.int32, (160, 208), 1)
        zi, yi = ri % 16, ri // 16
        for layer in range(4):
            ox = (0, 1, 1, 2)[layer]
            xrow = (8, 0, 8, 0)[layer]
            face_row = jnp.where(yi == 0, 160 + xrow + 7, jnp.where(yi == 9, 192 + xrow, 176 + xrow + yi - 1))
            low_col = jnp.where(zi > 0, ri - 1, jnp.where(gz == 1, face_row, -1))
            high_col = jnp.where(zi < 15, ri + 1, jnp.where(gz == 0, face_row, -1))
            low = jnp.where(ci == low_col, 1.0, 0.0).astype(BF16)
            high = jnp.where(ci == high_col, 1.0, 0.0).astype(BF16)
            cells = jnp.concatenate([field[layer].reshape(160, ch), received[ox].reshape(48, ch)], axis=0)
            shifted[0, layer] = jnp.dot(low, cells, preferred_element_type=F32).astype(BF16).reshape(10, 16, ch)
            shifted[2, layer] = jnp.dot(high, cells, preferred_element_type=F32).astype(BF16).reshape(10, 16, ch)

    def tap_of(t):
        t = jnp.minimum(t, 26)
        return t // 9, (t // 3) % 3, t % 3

    def g_window(t, field):
        dx, dy, dz = tap_of(t)
        return field[2 - dz, pl.ds(2 - dx, 2), pl.ds(2 - dy, 8)].reshape(256, 128)

    def x_window(t):
        dx, dy, dz = tap_of(t)
        return x3[dz, pl.ds(dx, 2), pl.ds(dy, 8)].reshape(256, 256)

    halo(slab, g_hbm, gc, 0, "wait_recv")
    halo(face, gface, gfr, 0, "wait_recv")
    share(1).start()
    share(2).start()
    shift_all(gc, gfr, g3)
    halo(slab, x_hbm, xc, 17, "start")
    halo(face, xface, xfr, 17, "start")
    for k in (1, 2, 0):
        share(k).wait_recv()
    shift_all(gc2, gfr2, g32)

    def to_x(g, d):
        return pltpu.make_async_remote_copy(
            x_send.at[g, d - 1], x_recv.at[g, d - 1], xs_s.at[g, d - 1], xs_r.at[g, d - 1],
            device_id=x_peers[d - 1], device_id_type=MESH)

    def to_b(d):
        return pltpu.make_async_remote_copy(
            b_send.at[d - 1], b_recv.at[d - 1], bs_s.at[d - 1], bs_r.at[d - 1],
            device_id=(((y + d) % 8) * 4 + zl, r), device_id_type=MESH)

    def to_bx(d):
        return pltpu.make_async_remote_copy(
            bx_send.at[d - 1], bx_recv.at[d - 1], bx_s.at[d - 1], bx_r.at[d - 1],
            device_id=x_peers[d - 1], device_id_type=MESH)

    def to_y(g):
        slot = (g - y + 8) % 8 - 1
        return pltpu.make_async_remote_copy(
            y_send.at[g], y_recv.at[slot], ys_s.at[g], ys_r.at[slot],
            device_id=(g * 4 + zl, r), device_id_type=MESH)

    def from_y(slot):
        return pltpu.make_async_remote_copy(
            y_send.at[0], y_recv.at[slot], ys_s.at[0], ys_r.at[slot],
            device_id=y_peers[1], device_id_type=MESH)

    def to_z(d):
        z_to = (z + d) % 8
        return pltpu.make_async_remote_copy(
            z_send.at[z_to // 4], z_recv.at[z], zs_s.at[d - 1], zs_r.at[z],
            device_id=z_peers[d], device_id_type=MESH)

    def from_z(d):
        z_from = (z + d) % 8
        return pltpu.make_async_remote_copy(
            z_send.at[0], z_recv.at[z_from], zs_s.at[0], zs_r.at[z_from],
            device_id=z_peers[d], device_id_type=MESH)

    def to_all(d):
        return pltpu.make_async_remote_copy(
            done.at[y], done.at[y], ag_s.at[d - 1], ag_r.at[y],
            device_id=y_peers[d], device_id_type=MESH)

    def from_owner(g):
        return pltpu.make_async_remote_copy(
            done.at[g], done.at[g], ag_s.at[0], ag_r.at[g],
            device_id=y_peers[1], device_id_type=MESH)

    def products(t):
        terms = jnp.zeros((128, 256), F32)
        for field, chans in ((g3, xt[:, c]), (g32, xt2[...])):
            both = jnp.concatenate([g_window(t, field), g_window(t + 1, field)], axis=1)
            terms = terms + jnp.dot(chans.reshape(128, 256), both, preferred_element_type=F32)
        return [terms[:, 128 * i : 128 * i + 128].reshape(2, 4, 16, 128) for i in range(2)]

    def step(i):
        dy = 4 + ((i + 1) // 2) * (1 - 2 * (i % 2))
        return dy, (y + dy) % 8

    def wgrad(i, carry):
        dy, q = step(i)

        @pl.when(q < GROUPS)
        def _():
            part_a[q, 2], part_b[...] = products(4 * q + 2)

            @pl.when(dy != 0)
            def _():
                encode(part_b[...].reshape(8, 16, 128), b_send.at[dy - 1])
                to_b(dy).start()

            part_a[q, 0], part_a[q, 1] = products(4 * q)
            for d in (2, 1, 3):
                encode(part_a[q, :, :, (x + d) % 4].reshape(6, 16, 128), x_send.at[q, d - 1])
                to_x(q, d).start()

        return carry

    lax.fori_loop(0, 8, wgrad, 0)
    loads[2].wait()
    acc_b[...] = jnp.zeros_like(acc_b)
    acc_f[...] = jnp.zeros_like(acc_f)

    def backward(t0, count):
        for t in range(0, count, 2):
            n = min(2, count - t)
            wins = [g_window(t0 + t + i, g3) for i in range(n)]
            kers = [wv[t0 + t + i] for i in range(n)]
            win = jnp.concatenate(wins, axis=1) if n == 2 else wins[0]
            ker = jnp.concatenate(kers, axis=1) if n == 2 else kers[0]
            acc_b[...] += lax.dot_general(win, ker, (((1,), (1,)), ((), ())), preferred_element_type=F32)

    def reduce(i, carry):
        dy, q = step(i)

        @pl.when(q < GROUPS)
        def _():
            for d in (1, 3, 2):
                to_x(q, d).wait_recv()
            total = part_a[q, :, :, x].reshape(6, 16, 128)
            for d in (1, 3, 2):
                total = total + decode(x_recv.at[q, d - 1], 6)

            @pl.when(dy == 0)
            def _():
                own_a[...] = total

            @pl.when(dy != 0)
            def _():
                encode(total, y_send.at[q])
                to_y(q).start()

        @pl.when(i < GROUPS)
        def _():
            backward(4 * i, 3)

        @pl.when(i < GROUPS - 1)
        def _():
            backward(4 * i + 3, 1)

        return carry

    lax.fori_loop(0, 8, reduce, 0)

    @pl.when(y < GROUPS)
    def _():
        total = part_b[...].reshape(8, 16, 128)
        for d in FAR_FIRST:
            to_b(d).wait_recv()
            total = total + decode(b_recv.at[d - 1], 8)
        part_b[...] = total.reshape(2, 4, 16, 128)
        for d in (2, 1, 3):
            encode(part_b[:, (x + d) % 4], bx_send.at[d - 1])
            to_bx(d).start()

    halo(slab, x_hbm, xc, 17, "wait_recv")
    halo(face, xface, xfr, 17, "wait_recv")
    shift_all(xc, xfr, x3)

    def forward(k, carry):
        for i in range(3):
            acc_f[...] += jnp.dot(x_window(3 * k + i), wv[3 * k + i], preferred_element_type=F32)
        return carry

    lax.fori_loop(0, 9, forward, 0)

    @pl.when(y < GROUPS)
    def _():
        first = own_a[...]
        for d in FAR_FIRST:
            from_y(d - 1).wait_recv()
            first = first + decode(y_recv.at[d - 1], 6)
        second = part_b[:, x]
        for d in (1, 2, 3):
            to_bx(d).wait_recv()
            second = second + decode(bx_recv.at[d - 1], 2)
        total = jnp.concatenate([first, second], axis=0).reshape(4, 2, 16, 128)
        for h in range(2):
            encode(total[:, h], z_send.at[h])
        for d in FAR_FIRST:
            to_z(d).start()
        z_recv[z] = z_send[zh]

    back_ref[...] = acc_b[...].astype(BF16).reshape(2, 8, 16, 256)
    out_ref[...] = acc_f[...].astype(BF16).reshape(2, 8, 16, 128)

    def sent(g, carry):
        for d in (1, 2, 3):
            to_x(g, d).wait_send()

        @pl.when(y != g)
        def _():
            to_y(g).wait_send()

        return carry

    lax.fori_loop(0, GROUPS, sent, 0)
    for k in range(3):
        share(k).wait_send()
    for d in range(1, 8):
        @pl.when((y + d) % 8 < GROUPS)
        def _(d=d):
            to_b(d).wait_send()
    for source, field, base in ((g_hbm, gc, 0), (x_hbm, xc, 17)):
        halo(slab, source, field, base, "wait_send")
    for source, field, base in ((gface, gfr, 0), (xface, xfr, 17)):
        halo(face, source, field, base, "wait_send")

    @pl.when(y < GROUPS)
    def _():
        for d in FAR_FIRST:
            from_z(d).wait_recv()
        total = decode(z_recv.at[0], 4)
        for k in range(1, 8):
            total = total + decode(z_recv.at[k], 4)
        encode(total / jnp.sqrt(F32(131072)), done.at[y])
        for d in FAR_FIRST:
            to_all(d).start()
        for d in FAR_FIRST:
            to_z(d).wait_send()
        for d in (1, 2, 3):
            to_bx(d).wait_send()

    def arrived(g, carry):
        @pl.when(y != g)
        def _():
            from_owner(g).wait_recv()

        kg_ref[g] = decode(done.at[g], 4)
        return carry

    lax.fori_loop(0, GROUPS, arrived, 0)

    @pl.when(y < GROUPS)
    def _():
        for d in FAR_FIRST:
            to_all(d).wait_send()


def per_device(volumes, weights, out_grads):
    vm = pltpu.VMEM
    dma = pltpu.SemaphoreType.DMA
    in_hbm = pl.BlockSpec(memory_space=pltpu.HBM)
    in_vmem = pl.BlockSpec(memory_space=pltpu.VMEM)
    out, back, kg = pl.pallas_call(
        kernel,
        out_shape=(
            jax.ShapeDtypeStruct((2, 8, 16, 128), BF16),
            jax.ShapeDtypeStruct((2, 8, 16, 256), BF16),
            jax.ShapeDtypeStruct((GROUPS, 4, 16, 128), F32),
        ),
        in_specs=[in_hbm] * 3,
        out_specs=(in_vmem,) * 3,
        scratch_shapes=[
            vm((27, 256, 128), BF16), vm((4, 10, 16, 256), BF16), vm((4, 10, 16, 128), BF16), vm((4, 10, 16, 128), BF16),
            vm((3, 4, 10, 16, 256), BF16), vm((3, 4, 10, 16, 128), BF16), vm((3, 4, 10, 16, 128), BF16),
            vm((16, 256), BF16), vm((16, 128), BF16), vm((3, 3, 16, 256), BF16), vm((3, 3, 16, 128), BF16),
            vm((3, 3, 16, 128), BF16), vm((8, 2, 16, 256), BF16), vm((8, 16, 256), BF16),
            vm((GROUPS, 3, 2, 4, 16, 128), F32), vm((2, 4, 16, 128), F32),
            vm((GROUPS, 3, 7, 16, 128), BF16), vm((GROUPS, 3, 7, 16, 128), BF16), vm((6, 16, 128), F32),
            vm((GROUPS, 7, 16, 128), BF16), vm((7, 7, 16, 128), BF16),
            vm((7, 9, 16, 128), BF16), vm((7, 9, 16, 128), BF16),
            vm((3, 3, 16, 128), BF16), vm((3, 3, 16, 128), BF16),
            vm((2, 5, 16, 128), BF16), vm((8, 5, 16, 128), BF16), vm((GROUPS, 5, 16, 128), BF16),
            vm((256, 128), F32), vm((256, 256), F32),
            dma((3,)), dma((34,)), dma((34,)), dma((3,)), dma((3,)),
            dma((GROUPS, 3)), dma((GROUPS, 3)), dma((GROUPS,)), dma((7,)),
            dma((7,)), dma((7,)), dma((3,)), dma((3,)), dma((7,)), dma((8,)),
            dma((7,)), dma((GROUPS,)),
        ],
        compiler_params=pltpu.CompilerParams(
            collective_id=0, has_side_effects=True, vmem_limit_bytes=40 * 2**20),
        cost_estimate=pl.CostEstimate(flops=1400000000, bytes_accessed=3000000, transcendentals=0),
    )(*(pltpu.with_memory_space_constraint(array, pltpu.HBM) for array in (
        volumes.reshape(2, 8, 16, 256), weights.reshape(27, 256, 128), out_grads.reshape(2, 8, 16, 128))))
    kg = kg.reshape(28, 16, 128)[:27].reshape(3, 3, 3, 16, 128)
    return out[None, None], back[None, None], kg


def solution(mesh):
    block = P("replica", "space", None, None, None, None)
    return jax.shard_map(
        per_device, mesh=mesh, in_specs=(block, P(), block),
        out_specs=(block, block, P(None, None, None, "replica", None)), check_vma=False)
```

```python
import jax
import jax.numpy as jnp
from jax import lax
from jax.experimental import pallas as pl
from jax.experimental.pallas import tpu as pltpu
from jax.sharding import PartitionSpec as P

MESH = pl.DeviceIdType.MESH
F32 = jnp.float32
BF16 = jnp.bfloat16
GROUPS = 7
FAR_FIRST = (4, 3, 5, 2, 6, 1, 7)
LIFT = 32768.0
PLANE = [(-1, -1), (-1, 1), (1, -1), (1, 1), (-1, 0), (1, 0), (0, -1), (0, 1), (0, 0)]


def encode(u, msg):
    n = u.shape[0]
    top = jnp.max(jnp.max(jnp.abs(u), axis=0), axis=0, keepdims=True)
    top = jnp.maximum(top, 1e-30).astype(BF16)
    v = u * (LIFT / top.astype(F32))
    v2 = v * v
    v4 = v2 * v2
    msg[pl.ds(0, n)] = ((v4 * v2) * (v * jnp.abs(v))).astype(BF16)
    msg[n] = jnp.broadcast_to(top.astype(F32), (16, 128)).astype(BF16)


def decode(msg, n):
    y = msg[pl.ds(0, n)].astype(F32)
    scale = msg[n].astype(F32) * (1.0 / LIFT)
    a = jnp.abs(y)
    t = lax.rsqrt(lax.rsqrt(a))
    u = jnp.where(a == 0.0, 0.0, t * lax.rsqrt(t))
    return jnp.where(y < 0.0, -u, u) * scale


def kernel(
    x_hbm, w_hbm, g_hbm, out_ref, back_ref, kg_ref,
    wv, xc, gc, gc2, x3, g3, g32, xface, gface, xfr, gfr, gfr2, xt, xt2,
    part_a, part_b, x_send, x_recv, own_a, y_send, y_recv, b_send, b_recv, bx_send, bx_recv,
    z_send, z_recv, done, acc_f, acc_b,
    in_sem, halo_s, halo_r, sib_s, sib_r, xs_s, xs_r, ys_s, ys_r, bs_s, bs_r, bx_s, bx_r, zs_s, zs_r, ag_s, ag_r,
):
    s = lax.axis_index("space")
    r = lax.axis_index("replica")
    y, zl = s // 4, s % 4
    zh, x, c = r // 8, (r // 2) % 4, r % 2
    gx, gy, gz = s // 8, (s // 2) % 4, s % 2

    loads = [
        pltpu.make_async_copy(g_hbm, gc.at[pl.ds(1, 2), pl.ds(1, 8)], in_sem.at[0]),
        pltpu.make_async_copy(x_hbm, xc.at[pl.ds(1, 2), pl.ds(1, 8)], in_sem.at[1]),
        pltpu.make_async_copy(w_hbm, wv, in_sem.at[2]),
    ]
    for load in loads:
        load.start()
    for field in (gc, xc):
        none = jnp.zeros((1, 10, 16, field.shape[3]), BF16)
        field[pl.ds(0, 1)] = none
        field[pl.ds(3, 1)] = none
        none = jnp.zeros((2, 1, 16, field.shape[3]), BF16)
        field[pl.ds(1, 2), pl.ds(0, 1)] = none
        field[pl.ds(1, 2), pl.ds(9, 1)] = none
    gfr[...] = jnp.zeros_like(gfr)
    xfr[...] = jnp.zeros_like(xfr)

    def inside(ox, oy):
        return (gx + ox >= 0) & (gx + ox <= 3) & (gy + oy >= 0) & (gy + oy <= 3)

    def at(ox, oy, other):
        return ((gx + ox) * 8 + (gy + oy) * 2 + (1 - gz if other else gz), r)

    z = zh * 4 + zl
    sibling = (s, r + 1 - 2 * c)
    x_peers = [(s, zh * 8 + ((x + d) % 4) * 2 + c) for d in (1, 2, 3)]
    y_peers = {d: (((y + d) % 8) * 4 + zl, r) for d in FAR_FIRST}

    def z_peer(d):
        z_to = (z + d) % 8
        return (y * 4 + z_to % 4, (z_to // 4) * 8 + x * 2 + c)

    z_peers = {d: z_peer(d) for d in FAR_FIRST}

    barrier = pltpu.get_barrier_semaphore()

    def greet(who):
        pl.semaphore_signal(barrier, inc=1, device_id=who, device_id_type=MESH)

    expected = 18
    for ox, oy in PLANE:
        here = inside(ox, oy)
        if (ox, oy) == (0, 0):
            greet(at(0, 0, True))
            expected = expected + 1
            continue

        @pl.when(here)
        def _(ox=ox, oy=oy):
            greet(at(ox, oy, False))
            greet(at(ox, oy, True))

        expected = expected + jnp.where(here, 2, 0)
    for who in x_peers + list(y_peers.values()) + list(z_peers.values()) + [sibling]:
        greet(who)

    def cut(o, size):
        return (pl.ds(0, size), pl.ds(1, size)) if o == 0 else (
            (pl.ds(size - 1, 1), pl.ds(0, 1)) if o == 1 else (pl.ds(0, 1), pl.ds(size + 1, 1)))

    def slab(source, field, k, ox, oy, base):
        (xs, xd), (ys, yd) = cut(ox, 2), cut(oy, 8)
        return pltpu.make_async_remote_copy(
            source.at[xs, ys], field.at[xd, yd], halo_s.at[base + k], halo_r.at[base + k],
            device_id=at(ox, oy, False), device_id_type=MESH)

    def face(source, field, k, ox, oy, base):
        return pltpu.make_async_remote_copy(
            source, field.at[1 - ox, 1 - oy], halo_s.at[base + 8 + k], halo_r.at[base + 8 + k],
            device_id=at(ox, oy, True), device_id_type=MESH)

    def halo(message, source, field, base, do):
        for k, (ox, oy) in enumerate(PLANE):
            here = inside(-ox, -oy) if do == "wait_recv" else inside(ox, oy)
            if (ox, oy) == (0, 0):
                if message is face:
                    getattr(message(source, field, k, ox, oy, base), do)()
                continue

            @pl.when(here)
            def _(k=k, ox=ox, oy=oy):
                getattr(message(source, field, k, ox, oy, base), do)()

    def share(k):
        source, target = ((xt.at[:, 1 - c], xt2), (gc, gc2), (gfr, gfr2))[k]
        return pltpu.make_async_remote_copy(
            source, target, sib_s.at[k], sib_r.at[k], device_id=sibling, device_id_type=MESH)

    rows = lax.broadcasted_iota(jnp.int32, (16, 256), 0)
    cols = lax.broadcasted_iota(jnp.int32, (16, 256), 1)
    pick = jnp.where(cols == rows * 16 + jnp.where(gz == 0, 15, 0), 1.0, 0.0).astype(BF16)

    def interior(field):
        return field[pl.ds(1, 2), pl.ds(1, 8)].reshape(256, field.shape[3])

    pl.semaphore_wait(barrier, expected)
    halo(slab, g_hbm, gc, 0, "start")
    loads[0].wait()
    gface[...] = jnp.dot(pick, interior(gc), preferred_element_type=F32).astype(BF16)
    halo(face, gface, gfr, 0, "start")
    loads[1].wait()
    xface[...] = jnp.dot(pick, interior(xc), preferred_element_type=F32).astype(BF16)
    xt[...] = interior(xc).T.reshape(8, 2, 16, 256)
    share(0).start()

    def shift_all(field, received, shifted):
        ch = field.shape[3]
        shifted[1] = field[...]
        ri = lax.broadcasted_iota(jnp.int32, (160, 208), 0)
        ci = lax.broadcasted_iota(jnp.int32, (160, 208), 1)
        zi, yi = ri % 16, ri // 16
        for layer in range(4):
            ox = (0, 1, 1, 2)[layer]
            xrow = (8, 0, 8, 0)[layer]
            face_row = jnp.where(yi == 0, 160 + xrow + 7, jnp.where(yi == 9, 192 + xrow, 176 + xrow + yi - 1))
            low_col = jnp.where(zi > 0, ri - 1, jnp.where(gz == 1, face_row, -1))
            high_col = jnp.where(zi < 15, ri + 1, jnp.where(gz == 0, face_row, -1))
            low = jnp.where(ci == low_col, 1.0, 0.0).astype(BF16)
            high = jnp.where(ci == high_col, 1.0, 0.0).astype(BF16)
            cells = jnp.concatenate([field[layer].reshape(160, ch), received[ox].reshape(48, ch)], axis=0)
            shifted[0, layer] = jnp.dot(low, cells, preferred_element_type=F32).astype(BF16).reshape(10, 16, ch)
            shifted[2, layer] = jnp.dot(high, cells, preferred_element_type=F32).astype(BF16).reshape(10, 16, ch)

    def tap_of(t):
        t = jnp.minimum(t, 26)
        return t // 9, (t // 3) % 3, t % 3

    def g_window(t, field):
        dx, dy, dz = tap_of(t)
        return field[2 - dz, pl.ds(2 - dx, 2), pl.ds(2 - dy, 8)].reshape(256, 128)

    def x_window(t):
        dx, dy, dz = tap_of(t)
        return x3[dz, pl.ds(dx, 2), pl.ds(dy, 8)].reshape(256, 256)

    halo(slab, g_hbm, gc, 0, "wait_recv")
    halo(face, gface, gfr, 0, "wait_recv")
    share(1).start()
    share(2).start()
    shift_all(gc, gfr, g3)
    halo(slab, x_hbm, xc, 17, "start")
    halo(face, xface, xfr, 17, "start")
    for k in (1, 2, 0):
        share(k).wait_recv()
    shift_all(gc2, gfr2, g32)

    def to_x(g, d):
        return pltpu.make_async_remote_copy(
            x_send.at[g, d - 1], x_recv.at[g, d - 1], xs_s.at[g, d - 1], xs_r.at[g, d - 1],
            device_id=x_peers[d - 1], device_id_type=MESH)

    def to_b(d):
        return pltpu.make_async_remote_copy(
            b_send.at[d - 1], b_recv.at[d - 1], bs_s.at[d - 1], bs_r.at[d - 1],
            device_id=(((y + d) % 8) * 4 + zl, r), device_id_type=MESH)

    def to_bx(d):
        return pltpu.make_async_remote_copy(
            bx_send.at[d - 1], bx_recv.at[d - 1], bx_s.at[d - 1], bx_r.at[d - 1],
            device_id=x_peers[d - 1], device_id_type=MESH)

    def to_y(g):
        slot = (g - y + 8) % 8 - 1
        return pltpu.make_async_remote_copy(
            y_send.at[g], y_recv.at[slot], ys_s.at[g], ys_r.at[slot],
            device_id=(g * 4 + zl, r), device_id_type=MESH)

    def from_y(slot):
        return pltpu.make_async_remote_copy(
            y_send.at[0], y_recv.at[slot], ys_s.at[0], ys_r.at[slot],
            device_id=y_peers[1], device_id_type=MESH)

    def to_z(d):
        z_to = (z + d) % 8
        return pltpu.make_async_remote_copy(
            z_send.at[z_to // 4], z_recv.at[z], zs_s.at[d - 1], zs_r.at[z],
            device_id=z_peers[d], device_id_type=MESH)

    def from_z(d):
        z_from = (z + d) % 8
        return pltpu.make_async_remote_copy(
            z_send.at[0], z_recv.at[z_from], zs_s.at[0], zs_r.at[z_from],
            device_id=z_peers[d], device_id_type=MESH)

    def to_all(d):
        return pltpu.make_async_remote_copy(
            done.at[y], done.at[y], ag_s.at[d - 1], ag_r.at[y],
            device_id=y_peers[d], device_id_type=MESH)

    def from_owner(g):
        return pltpu.make_async_remote_copy(
            done.at[g], done.at[g], ag_s.at[0], ag_r.at[g],
            device_id=y_peers[1], device_id_type=MESH)

    def products(t):
        terms = jnp.zeros((128, 256), F32)
        for field, chans in ((g3, xt[:, c]), (g32, xt2[...])):
            both = jnp.concatenate([g_window(t, field), g_window(t + 1, field)], axis=1)
            terms = terms + jnp.dot(chans.reshape(128, 256), both, preferred_element_type=F32)
        return [terms[:, 128 * i : 128 * i + 128].reshape(2, 4, 16, 128) for i in range(2)]

    def step(i):
        dy = 4 + ((i + 1) // 2) * (1 - 2 * (i % 2))
        return dy, (y + dy) % 8

    def wgrad(i, carry):
        dy, q = step(i)

        @pl.when(q < GROUPS)
        def _():
            part_a[q, 2], part_b[...] = products(4 * q + 2)

            @pl.when(dy != 0)
            def _():
                encode(part_b[...].reshape(8, 16, 128), b_send.at[dy - 1])
                to_b(dy).start()

            part_a[q, 0], part_a[q, 1] = products(4 * q)
            for d in (2, 1, 3):
                encode(part_a[q, :, :, (x + d) % 4].reshape(6, 16, 128), x_send.at[q, d - 1])
                to_x(q, d).start()

        return carry

    lax.fori_loop(0, 8, wgrad, 0)
    loads[2].wait()
    acc_b[...] = jnp.zeros_like(acc_b)
    acc_f[...] = jnp.zeros_like(acc_f)

    def backward(t0, count):
        for t in range(0, count, 2):
            n = min(2, count - t)
            wins = [g_window(t0 + t + i, g3) for i in range(n)]
            kers = [wv[t0 + t + i] for i in range(n)]
            win = jnp.concatenate(wins, axis=1) if n == 2 else wins[0]
            ker = jnp.concatenate(kers, axis=1) if n == 2 else kers[0]
            acc_b[...] += lax.dot_general(win, ker, (((1,), (1,)), ((), ())), preferred_element_type=F32)

    def reduce(i, carry):
        dy, q = step(i)

        @pl.when(q < GROUPS)
        def _():
            for d in (1, 3, 2):
                to_x(q, d).wait_recv()
            total = part_a[q, :, :, x].reshape(6, 16, 128)
            for d in (1, 3, 2):
                total = total + decode(x_recv.at[q, d - 1], 6)

            @pl.when(dy == 0)
            def _():
                own_a[...] = total

            @pl.when(dy != 0)
            def _():
                encode(total, y_send.at[q])
                to_y(q).start()

        @pl.when(i < GROUPS)
        def _():
            backward(4 * i, 3)

        @pl.when(i < GROUPS - 1)
        def _():
            backward(4 * i + 3, 1)

        return carry

    lax.fori_loop(0, 8, reduce, 0)

    @pl.when(y < GROUPS)
    def _():
        total = part_b[...].reshape(8, 16, 128)
        for d in FAR_FIRST:
            to_b(d).wait_recv()
            total = total + decode(b_recv.at[d - 1], 8)
        part_b[...] = total.reshape(2, 4, 16, 128)
        for d in (2, 1, 3):
            encode(part_b[:, (x + d) % 4], bx_send.at[d - 1])
            to_bx(d).start()

    halo(slab, x_hbm, xc, 17, "wait_recv")
    halo(face, xface, xfr, 17, "wait_recv")
    shift_all(xc, xfr, x3)

    @pl.when(y < GROUPS)
    def _():
        first = own_a[...]
        for d in FAR_FIRST:
            from_y(d - 1).wait_recv()
            first = first + decode(y_recv.at[d - 1], 6)
        second = part_b[:, x]
        for d in (1, 2, 3):
            to_bx(d).wait_recv()
            second = second + decode(bx_recv.at[d - 1], 2)
        total = jnp.concatenate([first, second], axis=0).reshape(4, 2, 16, 128)
        for h in range(2):
            encode(total[:, h], z_send.at[h])
        for d in FAR_FIRST:
            to_z(d).start()
        z_recv[z] = z_send[zh]

    def forward(k, carry):
        for i in range(3):
            acc_f[...] += jnp.dot(x_window(3 * k + i), wv[3 * k + i], preferred_element_type=F32)
        return carry

    lax.fori_loop(0, 9, forward, 0)

    back_ref[...] = acc_b[...].astype(BF16).reshape(2, 8, 16, 256)
    out_ref[...] = acc_f[...].astype(BF16).reshape(2, 8, 16, 128)

    @pl.when(y < GROUPS)
    def _():
        for d in FAR_FIRST:
            from_z(d).wait_recv()
        total = decode(z_recv.at[0], 4)
        for k in range(1, 8):
            total = total + decode(z_recv.at[k], 4)
        encode(total / jnp.sqrt(F32(131072)), done.at[y])
        for d in FAR_FIRST:
            to_all(d).start()
        for d in FAR_FIRST:
            to_z(d).wait_send()
        for d in (1, 2, 3):
            to_bx(d).wait_send()

    def sent(g, carry):
        for d in (1, 2, 3):
            to_x(g, d).wait_send()

        @pl.when(y != g)
        def _():
            to_y(g).wait_send()

        return carry

    lax.fori_loop(0, GROUPS, sent, 0)
    for k in range(3):
        share(k).wait_send()
    for d in range(1, 8):
        @pl.when((y + d) % 8 < GROUPS)
        def _(d=d):
            to_b(d).wait_send()
    for source, field, base in ((g_hbm, gc, 0), (x_hbm, xc, 17)):
        halo(slab, source, field, base, "wait_send")
    for source, field, base in ((gface, gfr, 0), (xface, xfr, 17)):
        halo(face, source, field, base, "wait_send")

    def arrived(g, carry):
        @pl.when(y != g)
        def _():
            from_owner(g).wait_recv()

        kg_ref[g] = decode(done.at[g], 4)
        return carry

    lax.fori_loop(0, GROUPS, arrived, 0)

    @pl.when(y < GROUPS)
    def _():
        for d in FAR_FIRST:
            to_all(d).wait_send()


def per_device(volumes, weights, out_grads):
    vm = pltpu.VMEM
    dma = pltpu.SemaphoreType.DMA
    in_hbm = pl.BlockSpec(memory_space=pltpu.HBM)
    in_vmem = pl.BlockSpec(memory_space=pltpu.VMEM)
    out, back, kg = pl.pallas_call(
        kernel,
        out_shape=(
            jax.ShapeDtypeStruct((2, 8, 16, 128), BF16),
            jax.ShapeDtypeStruct((2, 8, 16, 256), BF16),
            jax.ShapeDtypeStruct((GROUPS, 4, 16, 128), F32),
        ),
        in_specs=[in_hbm] * 3,
        out_specs=(in_vmem,) * 3,
        scratch_shapes=[
            vm((27, 256, 128), BF16), vm((4, 10, 16, 256), BF16), vm((4, 10, 16, 128), BF16), vm((4, 10, 16, 128), BF16),
            vm((3, 4, 10, 16, 256), BF16), vm((3, 4, 10, 16, 128), BF16), vm((3, 4, 10, 16, 128), BF16),
            vm((16, 256), BF16), vm((16, 128), BF16), vm((3, 3, 16, 256), BF16), vm((3, 3, 16, 128), BF16),
            vm((3, 3, 16, 128), BF16), vm((8, 2, 16, 256), BF16), vm((8, 16, 256), BF16),
            vm((GROUPS, 3, 2, 4, 16, 128), F32), vm((2, 4, 16, 128), F32),
            vm((GROUPS, 3, 7, 16, 128), BF16), vm((GROUPS, 3, 7, 16, 128), BF16), vm((6, 16, 128), F32),
            vm((GROUPS, 7, 16, 128), BF16), vm((7, 7, 16, 128), BF16),
            vm((7, 9, 16, 128), BF16), vm((7, 9, 16, 128), BF16),
            vm((3, 3, 16, 128), BF16), vm((3, 3, 16, 128), BF16),
            vm((2, 5, 16, 128), BF16), vm((8, 5, 16, 128), BF16), vm((GROUPS, 5, 16, 128), BF16),
            vm((256, 128), F32), vm((256, 256), F32),
            dma((3,)), dma((34,)), dma((34,)), dma((3,)), dma((3,)),
            dma((GROUPS, 3)), dma((GROUPS, 3)), dma((GROUPS,)), dma((7,)),
            dma((7,)), dma((7,)), dma((3,)), dma((3,)), dma((7,)), dma((8,)),
            dma((7,)), dma((GROUPS,)),
        ],
        compiler_params=pltpu.CompilerParams(
            collective_id=0, has_side_effects=True, vmem_limit_bytes=40 * 2**20),
        cost_estimate=pl.CostEstimate(flops=1400000000, bytes_accessed=3000000, transcendentals=0),
    )(*(pltpu.with_memory_space_constraint(array, pltpu.HBM) for array in (
        volumes.reshape(2, 8, 16, 256), weights.reshape(27, 256, 128), out_grads.reshape(2, 8, 16, 128))))
    kg = kg.reshape(28, 16, 128)[:27].reshape(3, 3, 3, 16, 128)
    return out[None, None], back[None, None], kg


def solution(mesh):
    block = P("replica", "space", None, None, None, None)
    return jax.shard_map(
        per_device, mesh=mesh, in_specs=(block, P(), block),
        out_specs=(block, block, P(None, None, None, "replica", None)), check_vma=False)
```

```python
import jax
import jax.numpy as jnp
from jax import lax
from jax.experimental import pallas as pl
from jax.experimental.pallas import tpu as pltpu
from jax.sharding import PartitionSpec as P

MESH = pl.DeviceIdType.MESH
F32 = jnp.float32
BF16 = jnp.bfloat16
GROUPS = 7
FAR_FIRST = (4, 3, 5, 2, 6, 1, 7)
LIFT = 32768.0
PLANE = [(-1, -1), (-1, 1), (1, -1), (1, 1), (-1, 0), (1, 0), (0, -1), (0, 1), (0, 0)]


def encode(u, msg):
    n = u.shape[0]
    top = jnp.max(jnp.max(jnp.abs(u), axis=0), axis=0, keepdims=True)
    top = jnp.maximum(top, 1e-30).astype(BF16)
    v = u * (LIFT / top.astype(F32))
    v2 = v * v
    v4 = v2 * v2
    msg[pl.ds(0, n)] = ((v4 * v2) * (v * jnp.abs(v))).astype(BF16)
    msg[n] = jnp.broadcast_to(top.astype(F32), (16, 128)).astype(BF16)


def decode(msg, n):
    y = msg[pl.ds(0, n)].astype(F32)
    scale = msg[n].astype(F32) * (1.0 / LIFT)
    a = jnp.abs(y)
    t = lax.rsqrt(lax.rsqrt(a))
    u = jnp.where(a == 0.0, 0.0, t * lax.rsqrt(t))
    return jnp.where(y < 0.0, -u, u) * scale


def kernel(
    x_hbm, w_hbm, g_hbm, out_ref, back_ref, kg_ref,
    wv, xc, gc, gc2, x3, g3, g32, xface, gface, xfr, gfr, gfr2, xt, xt2,
    part_a, x_send, x_recv, own_a, y_send, y_recv,
    z_send, z_recv, done, acc_f, acc_b,
    in_sem, halo_s, halo_r, sib_s, sib_r, xs_s, xs_r, ys_s, ys_r, zs_s, zs_r, ag_s, ag_r,
):
    s = lax.axis_index("space")
    r = lax.axis_index("replica")
    y, zl = s // 4, s % 4
    zh, x, c = r // 8, (r // 2) % 4, r % 2
    gx, gy, gz = s // 8, (s // 2) % 4, s % 2

    loads = [
        pltpu.make_async_copy(g_hbm, gc.at[pl.ds(1, 2), pl.ds(1, 8)], in_sem.at[0]),
        pltpu.make_async_copy(x_hbm, xc.at[pl.ds(1, 2), pl.ds(1, 8)], in_sem.at[1]),
        pltpu.make_async_copy(w_hbm, wv, in_sem.at[2]),
    ]
    for load in loads:
        load.start()
    for field in (gc, xc):
        none = jnp.zeros((1, 10, 16, field.shape[3]), BF16)
        field[pl.ds(0, 1)] = none
        field[pl.ds(3, 1)] = none
        none = jnp.zeros((2, 1, 16, field.shape[3]), BF16)
        field[pl.ds(1, 2), pl.ds(0, 1)] = none
        field[pl.ds(1, 2), pl.ds(9, 1)] = none
    gfr[...] = jnp.zeros_like(gfr)
    xfr[...] = jnp.zeros_like(xfr)

    def inside(ox, oy):
        return (gx + ox >= 0) & (gx + ox <= 3) & (gy + oy >= 0) & (gy + oy <= 3)

    def at(ox, oy, other):
        return ((gx + ox) * 8 + (gy + oy) * 2 + (1 - gz if other else gz), r)

    z = zh * 4 + zl
    sibling = (s, r + 1 - 2 * c)
    x_peers = [(s, zh * 8 + ((x + d) % 4) * 2 + c) for d in (1, 2, 3)]
    y_peers = {d: (((y + d) % 8) * 4 + zl, r) for d in FAR_FIRST}

    def z_peer(d):
        z_to = (z + d) % 8
        return (y * 4 + z_to % 4, (z_to // 4) * 8 + x * 2 + c)

    z_peers = {d: z_peer(d) for d in FAR_FIRST}

    barrier = pltpu.get_barrier_semaphore()

    def greet(who):
        pl.semaphore_signal(barrier, inc=1, device_id=who, device_id_type=MESH)

    expected = 18
    for ox, oy in PLANE:
        here = inside(ox, oy)
        if (ox, oy) == (0, 0):
            greet(at(0, 0, True))
            expected = expected + 1
            continue

        @pl.when(here)
        def _(ox=ox, oy=oy):
            greet(at(ox, oy, False))
            greet(at(ox, oy, True))

        expected = expected + jnp.where(here, 2, 0)
    for who in x_peers + list(y_peers.values()) + list(z_peers.values()) + [sibling]:
        greet(who)

    def cut(o, size):
        return (pl.ds(0, size), pl.ds(1, size)) if o == 0 else (
            (pl.ds(size - 1, 1), pl.ds(0, 1)) if o == 1 else (pl.ds(0, 1), pl.ds(size + 1, 1)))

    def slab(source, field, k, ox, oy, base):
        (xs, xd), (ys, yd) = cut(ox, 2), cut(oy, 8)
        return pltpu.make_async_remote_copy(
            source.at[xs, ys], field.at[xd, yd], halo_s.at[base + k], halo_r.at[base + k],
            device_id=at(ox, oy, False), device_id_type=MESH)

    def face(source, field, k, ox, oy, base):
        return pltpu.make_async_remote_copy(
            source, field.at[1 - ox, 1 - oy], halo_s.at[base + 8 + k], halo_r.at[base + 8 + k],
            device_id=at(ox, oy, True), device_id_type=MESH)

    def halo(message, source, field, base, do):
        for k, (ox, oy) in enumerate(PLANE):
            here = inside(-ox, -oy) if do == "wait_recv" else inside(ox, oy)
            if (ox, oy) == (0, 0):
                if message is face:
                    getattr(message(source, field, k, ox, oy, base), do)()
                continue

            @pl.when(here)
            def _(k=k, ox=ox, oy=oy):
                getattr(message(source, field, k, ox, oy, base), do)()

    def share(k):
        source, target = ((xt.at[:, 1 - c], xt2), (gc, gc2), (gfr, gfr2))[k]
        return pltpu.make_async_remote_copy(
            source, target, sib_s.at[k], sib_r.at[k], device_id=sibling, device_id_type=MESH)

    rows = lax.broadcasted_iota(jnp.int32, (16, 256), 0)
    cols = lax.broadcasted_iota(jnp.int32, (16, 256), 1)
    pick = jnp.where(cols == rows * 16 + jnp.where(gz == 0, 15, 0), 1.0, 0.0).astype(BF16)

    def interior(field):
        return field[pl.ds(1, 2), pl.ds(1, 8)].reshape(256, field.shape[3])

    pl.semaphore_wait(barrier, expected)
    halo(slab, g_hbm, gc, 0, "start")
    loads[0].wait()
    gface[...] = jnp.dot(pick, interior(gc), preferred_element_type=F32).astype(BF16)
    halo(face, gface, gfr, 0, "start")
    loads[1].wait()
    xface[...] = jnp.dot(pick, interior(xc), preferred_element_type=F32).astype(BF16)
    xt[...] = interior(xc).T.reshape(8, 2, 16, 256)
    share(0).start()

    def shift_all(field, received, shifted):
        ch = field.shape[3]
        shifted[1] = field[...]
        ri = lax.broadcasted_iota(jnp.int32, (160, 208), 0)
        ci = lax.broadcasted_iota(jnp.int32, (160, 208), 1)
        zi, yi = ri % 16, ri // 16
        for layer in range(4):
            ox = (0, 1, 1, 2)[layer]
            xrow = (8, 0, 8, 0)[layer]
            face_row = jnp.where(yi == 0, 160 + xrow + 7, jnp.where(yi == 9, 192 + xrow, 176 + xrow + yi - 1))
            low_col = jnp.where(zi > 0, ri - 1, jnp.where(gz == 1, face_row, -1))
            high_col = jnp.where(zi < 15, ri + 1, jnp.where(gz == 0, face_row, -1))
            low = jnp.where(ci == low_col, 1.0, 0.0).astype(BF16)
            high = jnp.where(ci == high_col, 1.0, 0.0).astype(BF16)
            cells = jnp.concatenate([field[layer].reshape(160, ch), received[ox].reshape(48, ch)], axis=0)
            shifted[0, layer] = jnp.dot(low, cells, preferred_element_type=F32).astype(BF16).reshape(10, 16, ch)
            shifted[2, layer] = jnp.dot(high, cells, preferred_element_type=F32).astype(BF16).reshape(10, 16, ch)

    def tap_of(t):
        t = jnp.minimum(t, 26)
        return t // 9, (t // 3) % 3, t % 3

    def g_window(t, field):
        dx, dy, dz = tap_of(t)
        return field[2 - dz, pl.ds(2 - dx, 2), pl.ds(2 - dy, 8)].reshape(256, 128)

    def x_window(t):
        dx, dy, dz = tap_of(t)
        return x3[dz, pl.ds(dx, 2), pl.ds(dy, 8)].reshape(256, 256)

    halo(slab, g_hbm, gc, 0, "wait_recv")
    halo(face, gface, gfr, 0, "wait_recv")
    share(1).start()
    share(2).start()
    shift_all(gc, gfr, g3)
    halo(slab, x_hbm, xc, 17, "start")
    halo(face, xface, xfr, 17, "start")
    for k in (1, 2, 0):
        share(k).wait_recv()
    shift_all(gc2, gfr2, g32)

    def to_x(g, d):
        return pltpu.make_async_remote_copy(
            x_send.at[g, d - 1], x_recv.at[g, d - 1], xs_s.at[g, d - 1], xs_r.at[g, d - 1],
            device_id=x_peers[d - 1], device_id_type=MESH)

    def to_y(g):
        slot = (g - y + 8) % 8 - 1
        return pltpu.make_async_remote_copy(
            y_send.at[g], y_recv.at[slot], ys_s.at[g], ys_r.at[slot],
            device_id=(g * 4 + zl, r), device_id_type=MESH)

    def from_y(slot):
        return pltpu.make_async_remote_copy(
            y_send.at[0], y_recv.at[slot], ys_s.at[0], ys_r.at[slot],
            device_id=y_peers[1], device_id_type=MESH)

    def to_z(d):
        z_to = (z + d) % 8
        return pltpu.make_async_remote_copy(
            z_send.at[z_to // 4], z_recv.at[z], zs_s.at[d - 1], zs_r.at[z],
            device_id=z_peers[d], device_id_type=MESH)

    def from_z(d):
        z_from = (z + d) % 8
        return pltpu.make_async_remote_copy(
            z_send.at[0], z_recv.at[z_from], zs_s.at[0], zs_r.at[z_from],
            device_id=z_peers[d], device_id_type=MESH)

    def to_all(d):
        return pltpu.make_async_remote_copy(
            done.at[y], done.at[y], ag_s.at[d - 1], ag_r.at[y],
            device_id=y_peers[d], device_id_type=MESH)

    def from_owner(g):
        return pltpu.make_async_remote_copy(
            done.at[g], done.at[g], ag_s.at[0], ag_r.at[g],
            device_id=y_peers[1], device_id_type=MESH)

    def products(t):
        terms = jnp.zeros((128, 256), F32)
        for field, chans in ((g3, xt[:, c]), (g32, xt2[...])):
            both = jnp.concatenate([g_window(t, field), g_window(t + 1, field)], axis=1)
            terms = terms + jnp.dot(chans.reshape(128, 256), both, preferred_element_type=F32)
        return [terms[:, 128 * i : 128 * i + 128].reshape(2, 4, 16, 128) for i in range(2)]

    def step(i):
        dy = 4 + ((i + 1) // 2) * (1 - 2 * (i % 2))
        return dy, (y + dy) % 8

    def wgrad(i, carry):
        dy, q = step(i)

        @pl.when(q < GROUPS)
        def _():
            for k in (0, 2):
                part_a[q, k], part_a[q, k + 1] = products(4 * q + k)
            for d in (2, 1, 3):
                encode(part_a[q, :, :, (x + d) % 4].reshape(8, 16, 128), x_send.at[q, d - 1])
                to_x(q, d).start()

        return carry

    lax.fori_loop(0, 8, wgrad, 0)
    loads[2].wait()
    acc_b[...] = jnp.zeros_like(acc_b)
    acc_f[...] = jnp.zeros_like(acc_f)

    def backward(t0, count):
        for t in range(0, count, 2):
            n = min(2, count - t)
            wins = [g_window(t0 + t + i, g3) for i in range(n)]
            kers = [wv[t0 + t + i] for i in range(n)]
            win = jnp.concatenate(wins, axis=1) if n == 2 else wins[0]
            ker = jnp.concatenate(kers, axis=1) if n == 2 else kers[0]
            acc_b[...] += lax.dot_general(win, ker, (((1,), (1,)), ((), ())), preferred_element_type=F32)

    def reduce(i, carry):
        dy, q = step(i)

        @pl.when(q < GROUPS)
        def _():
            for d in (1, 3, 2):
                to_x(q, d).wait_recv()
            total = part_a[q, :, :, x].reshape(8, 16, 128)
            for d in (1, 3, 2):
                total = total + decode(x_recv.at[q, d - 1], 8)

            @pl.when(dy == 0)
            def _():
                own_a[...] = total

            @pl.when(dy != 0)
            def _():
                encode(total, y_send.at[q])
                to_y(q).start()

        @pl.when(i < GROUPS)
        def _():
            backward(4 * i, 3)

        @pl.when(i < GROUPS - 1)
        def _():
            backward(4 * i + 3, 1)

        return carry

    lax.fori_loop(0, 8, reduce, 0)

    halo(slab, x_hbm, xc, 17, "wait_recv")
    halo(face, xface, xfr, 17, "wait_recv")
    shift_all(xc, xfr, x3)

    @pl.when(y < GROUPS)
    def _():
        first = own_a[...]
        for d in FAR_FIRST:
            from_y(d - 1).wait_recv()
            first = first + decode(y_recv.at[d - 1], 8)
        total = first.reshape(4, 2, 16, 128)
        for h in range(2):
            encode(total[:, h], z_send.at[h])
        for d in FAR_FIRST:
            to_z(d).start()
        z_recv[z] = z_send[zh]

    def forward(k, carry):
        for i in range(3):
            acc_f[...] += jnp.dot(x_window(3 * k + i), wv[3 * k + i], preferred_element_type=F32)
        return carry

    lax.fori_loop(0, 9, forward, 0)

    back_ref[...] = acc_b[...].astype(BF16).reshape(2, 8, 16, 256)
    out_ref[...] = acc_f[...].astype(BF16).reshape(2, 8, 16, 128)

    @pl.when(y < GROUPS)
    def _():
        for d in FAR_FIRST:
            from_z(d).wait_recv()
        total = decode(z_recv.at[0], 4)
        for k in range(1, 8):
            total = total + decode(z_recv.at[k], 4)
        encode(total / jnp.sqrt(F32(131072)), done.at[y])
        for d in FAR_FIRST:
            to_all(d).start()
        for d in FAR_FIRST:
            to_z(d).wait_send()

    def sent(g, carry):
        for d in (1, 2, 3):
            to_x(g, d).wait_send()

        @pl.when(y != g)
        def _():
            to_y(g).wait_send()

        return carry

    lax.fori_loop(0, GROUPS, sent, 0)
    for k in range(3):
        share(k).wait_send()
    for source, field, base in ((g_hbm, gc, 0), (x_hbm, xc, 17)):
        halo(slab, source, field, base, "wait_send")
    for source, field, base in ((gface, gfr, 0), (xface, xfr, 17)):
        halo(face, source, field, base, "wait_send")

    def arrived(g, carry):
        @pl.when(y != g)
        def _():
            from_owner(g).wait_recv()

        kg_ref[g] = decode(done.at[g], 4)
        return carry

    lax.fori_loop(0, GROUPS, arrived, 0)

    @pl.when(y < GROUPS)
    def _():
        for d in FAR_FIRST:
            to_all(d).wait_send()


def per_device(volumes, weights, out_grads):
    vm = pltpu.VMEM
    dma = pltpu.SemaphoreType.DMA
    in_hbm = pl.BlockSpec(memory_space=pltpu.HBM)
    in_vmem = pl.BlockSpec(memory_space=pltpu.VMEM)
    out, back, kg = pl.pallas_call(
        kernel,
        out_shape=(
            jax.ShapeDtypeStruct((2, 8, 16, 128), BF16),
            jax.ShapeDtypeStruct((2, 8, 16, 256), BF16),
            jax.ShapeDtypeStruct((GROUPS, 4, 16, 128), F32),
        ),
        in_specs=[in_hbm] * 3,
        out_specs=(in_vmem,) * 3,
        scratch_shapes=[
            vm((27, 256, 128), BF16), vm((4, 10, 16, 256), BF16), vm((4, 10, 16, 128), BF16), vm((4, 10, 16, 128), BF16),
            vm((3, 4, 10, 16, 256), BF16), vm((3, 4, 10, 16, 128), BF16), vm((3, 4, 10, 16, 128), BF16),
            vm((16, 256), BF16), vm((16, 128), BF16), vm((3, 3, 16, 256), BF16), vm((3, 3, 16, 128), BF16),
            vm((3, 3, 16, 128), BF16), vm((8, 2, 16, 256), BF16), vm((8, 16, 256), BF16),
            vm((GROUPS, 4, 2, 4, 16, 128), F32),
            vm((GROUPS, 3, 9, 16, 128), BF16), vm((GROUPS, 3, 9, 16, 128), BF16), vm((8, 16, 128), F32),
            vm((GROUPS, 9, 16, 128), BF16), vm((7, 9, 16, 128), BF16),
            vm((2, 5, 16, 128), BF16), vm((8, 5, 16, 128), BF16), vm((GROUPS, 5, 16, 128), BF16),
            vm((256, 128), F32), vm((256, 256), F32),
            dma((3,)), dma((34,)), dma((34,)), dma((3,)), dma((3,)),
            dma((GROUPS, 3)), dma((GROUPS, 3)), dma((GROUPS,)), dma((7,)),
            dma((7,)), dma((8,)),
            dma((7,)), dma((GROUPS,)),
        ],
        compiler_params=pltpu.CompilerParams(
            collective_id=0, has_side_effects=True, vmem_limit_bytes=40 * 2**20),
        cost_estimate=pl.CostEstimate(flops=1400000000, bytes_accessed=3000000, transcendentals=0),
    )(*(pltpu.with_memory_space_constraint(array, pltpu.HBM) for array in (
        volumes.reshape(2, 8, 16, 256), weights.reshape(27, 256, 128), out_grads.reshape(2, 8, 16, 128))))
    kg = kg.reshape(28, 16, 128)[:27].reshape(3, 3, 3, 16, 128)
    return out[None, None], back[None, None], kg


def solution(mesh):
    block = P("replica", "space", None, None, None, None)
    return jax.shard_map(
        per_device, mesh=mesh, in_specs=(block, P(), block),
        out_specs=(block, block, P(None, None, None, "replica", None)), check_vma=False)
```
